32 devices in a mesh: group: 2 (over y), mem: 8 (over z, x), col: 2 (over core).
Axes of the slice: x: 2, y: 2, z: 4, core: 2. Of those that a mesh axis runs over, the one named last changes fastest.
Arguments:
- grads: bfloat16 [4096, 2048], P(('group', 'mem')), parts along dimension 0, may hold values from -6 to 6
- values: bfloat16 [4096, 512], P('mem', 'col'), may hold values from -0.25 to 0.25
- expand_weight: bfloat16 [4, 512, 2048], P(None, 'col', 'mem'), may hold values from -0.125 to 0.125
- row_factors: float32 [4096, 16], P(('group', 'mem')), parts along dimension 0, may hold values from -5 to 5
- col_factors: float32 [4096, 16], P(('group', 'mem')), parts along dimension 0, may hold values from -5 to 5
- core: float32 [2, 2], replicated, may hold values from -3 to 3
- pair_index: int32 [2, 2048], P(None, ('group', 'mem')), parts along dimension 1, may hold values from 0 to 16383, as said below
- counts: int32 [128], P(('group', 'mem')), parts along dimension 0, may hold values from 1 to 16, as said below
Outputs:
- value_grad: float32 [8192, 512], P(('group', 'mem'), 'col'), parts along dimension 0
- row_grad: float32 [4096, 16], P(('group', 'mem')), parts along dimension 0
- col_grad: float32 [4096, 16], P(('group', 'mem')), parts along dimension 0
- core_grad: float32 [4, 2], P('group'), parts along dimension 0
The draws below stay inside these ranges and needn't reach their ends.
There are 2 independent parts, one for each index of `group`. The reference program is written for one: setup_inputs(seed, part) draws one part's arguments, and reference() takes and returns one part's arrays. A program takes and returns all parts, laid end to end along the dimension named above; an argument that names none is the same for every part. Nothing has to cross between parts.
Inputs may be any that keep to these rules, and one draw needn't show every extreme that they name: `counts`: every block has at least 2 live rows; one owner has 16 live rows from every source, and each source fills one block completely. Padding rows hold zeros. Value rows lie below 512, tokens below 256. `pair_index`: row 0 lies below 16384, row 1 below 512.
All inputs are finite; a program needn't handle non-finite values.
Results may differ from the reference program's by a relative error of at most 0.0051.
Values may be sent and summed in bfloat16 or wider, within the bound.
No kernel may reach another device: no remote copies, remote signals or barrier semaphores. Data moves between devices by JAX's collectives and lax.ppermute only.
A program may use at most 64 MiB of HBM per device.

```python
import jax
import jax.numpy as jnp
from jax import lax

D = 2048
DV = 512
E = 4
RANK = 2
NR = 8
NC = 8
KC = 64
KR_DEV = 8
T_DEV = 256
CAP = 16
VR_DEV = 512
VROWS = 4096
TOKENS = 2048
N_MEM = 8


def owner_counts(key):
    key = jax.random.fold_in(key, 11)
    first, second, third, fourth = jax.random.split(key, 4)
    lowest = jax.random.randint(first, (N_MEM,), CAP // 2, 3 * CAP // 4 + 1)
    spread = jax.random.randint(second, (N_MEM, N_MEM), 0, 1 << 20)
    blocks = spread % (CAP + 1 - lowest[None, :]) + lowest[None, :]
    hottest = jax.random.randint(third, (N_MEM,), 0, N_MEM)
    blocks = blocks.at[jnp.arange(N_MEM), hottest].set(CAP)
    fullest = jax.random.randint(fourth, (), 0, N_MEM)
    blocks = blocks.at[:, fullest].set(CAP)
    return blocks.astype(jnp.int32)


def draw_counts(key, part):
    return owner_counts(key).reshape(N_MEM * N_MEM)


def draw_pair_index(key, part):
    blocks = owner_counts(key)
    key = jax.random.fold_in(key, 5)
    keys = jax.random.split(key, 5)
    shape = (N_MEM, N_MEM, CAP)
    token = jax.random.randint(keys[0], shape, 0, T_DEV)
    row_cand = jax.random.randint(keys[1], shape, 0, NR)
    col_cand = jax.random.randint(keys[2], shape, 0, NC)
    row_key = jax.random.randint(keys[3], shape, 0, KR_DEV)
    col_key = jax.random.randint(keys[4], shape, 0, KC)
    live = jnp.arange(CAP, dtype=jnp.int32)[None, None, :] < blocks[:, :, None]
    code = jnp.where(live, (token * NR + row_cand) * NC + col_cand, 0)
    local_row = jnp.where(live, row_key * KC + col_key, 0)
    code = code.at[0, 0, 0].set(T_DEV * NR * NC - 1)
    local_row = local_row.at[0, 0, 0].set(0)
    return jnp.stack([code.reshape(-1), local_row.reshape(-1)]).astype(jnp.int32)


def block_scale(stream_key, shape, cuts, least, top_value):
    def one(position, shards_of):
        steps = jax.random.uniform(jax.random.fold_in(jax.random.fold_in(stream_key, 6), position), (shards_of,), jnp.float32, least / len(cuts), top_value / len(cuts))
        return jnp.repeat(jnp.exp(steps), shape[position] // shards_of).reshape((-1,) + (1,) * (len(shape) - position - 1))

    level = one(*cuts[0])
    for cut in cuts[1:]:
        level = level * one(*cut)
    return level


def centred(rng, dims, width, limit, cuts=(), kind=jnp.bfloat16):
    result = width * jax.random.normal(rng, dims, jnp.float32)
    if cuts:
        result = result * block_scale(rng, dims, cuts, -0.22, 0.18)
    return jnp.clip(result, -limit, limit).astype(kind)


def setup_inputs(seed: int = 0, part: int = 0) -> dict:
    seeds = jax.random.split(jax.random.key(seed), 9)
    own_keys = jax.random.split(jax.random.fold_in(seeds[8], part), 9)
    grads = centred(own_keys[0], (TOKENS, D), 1.0, 6.0, ((0, 8),))
    values = centred(seeds[1], (VROWS, DV), DV ** -0.5, 0.25, ((0, 8), (1, 2)))
    expand_weight = centred(seeds[2], (E, DV, D), D ** -0.5, 0.125, ((1, 2), (2, 8)))
    row_factors = centred(own_keys[3], (TOKENS, NR * RANK), 1.0, 5.0, ((0, 8),), jnp.float32)
    col_factors = centred(own_keys[4], (TOKENS, NC * RANK), 1.0, 5.0, ((0, 8),), jnp.float32)
    core = centred(seeds[5], (RANK, RANK), 0.7, 3.0, (), jnp.float32)
    pair_index = draw_pair_index(jax.random.fold_in(jax.random.fold_in(seeds[8], part), 71), part)
    counts = draw_counts(jax.random.fold_in(jax.random.fold_in(seeds[8], part), 71), part)
    return dict(grads=grads, values=values, expand_weight=expand_weight, row_factors=row_factors, col_factors=col_factors, core=core, pair_index=pair_index, counts=counts)


def reference(grads, values, expand_weight, row_factors, col_factors, core, pair_index, counts):
    rows = N_MEM * CAP
    codes = pair_index[0].reshape(N_MEM, rows)
    locals_ = pair_index[1].reshape(N_MEM, rows)
    blocks = counts.reshape(N_MEM, N_MEM)
    weight = expand_weight.astype(jnp.float32)
    table = values.astype(jnp.float32)
    owner = jnp.repeat(jnp.arange(N_MEM, dtype=jnp.int32), CAP)
    within = jnp.tile(jnp.arange(CAP, dtype=jnp.int32), N_MEM)
    high = lax.Precision.HIGHEST

    def source(carry, index):
        value_grad, core_grad = carry
        start = (index * T_DEV).astype(jnp.int32)
        tok_grads = lax.dynamic_slice_in_dim(grads, start, T_DEV, 0).astype(jnp.float32)
        expanded = jnp.einsum("td,evd->tev", tok_grads, weight).astype(jnp.bfloat16)
        code = codes[index]
        local_row = locals_[index]
        live = within < blocks[index][owner]
        token = code // (NR * NC)
        row_cand = (code // NC) % NR
        col_cand = code % NC
        rfac = lax.dynamic_slice_in_dim(row_factors, start, T_DEV, 0).reshape(T_DEV, NR, RANK)
        cfac = lax.dynamic_slice_in_dim(col_factors, start, T_DEV, 0).reshape(T_DEV, NC, RANK)
        a_p = rfac[token, row_cand]
        b_p = cfac[token, col_cand]
        core_b = jnp.dot(b_p, core.T, precision=high)
        core_a = jnp.dot(a_p, core, precision=high)
        score = jnp.where(live, jnp.sum(a_p * core_b, -1), 0.0).astype(jnp.bfloat16)
        proj = (local_row % KC) % E
        pair_grad = jnp.where(live[:, None], expanded[token, proj], jnp.zeros((), jnp.bfloat16))
        contrib = (score.astype(jnp.float32)[:, None] * pair_grad.astype(jnp.float32)).astype(jnp.bfloat16)
        global_row = owner * VR_DEV + local_row
        value_grad = value_grad + jax.ops.segment_sum(contrib.astype(jnp.float32), global_row, num_segments=VROWS)
        dscore = jnp.sum(pair_grad.astype(jnp.float32) * table[global_row], -1)
        row_grad = jax.ops.segment_sum(dscore[:, None] * core_b, token * NR + row_cand, num_segments=T_DEV * NR)
        col_grad = jax.ops.segment_sum(dscore[:, None] * core_a, token * NC + col_cand, num_segments=T_DEV * NC)
        core_grad = core_grad + jnp.dot((dscore[:, None] * a_p).T, b_p, precision=high)
        return (value_grad, core_grad), (row_grad.reshape(T_DEV, NR * RANK), col_grad.reshape(T_DEV, NC * RANK))

    init = (jnp.zeros((VROWS, DV), jnp.float32), jnp.zeros((RANK, RANK), jnp.float32))
    (value_grad, core_grad), (row_grad, col_grad) = lax.scan(source, init, jnp.arange(N_MEM, dtype=jnp.int32))
    return value_grad, row_grad.reshape(TOKENS, NR * RANK), col_grad.reshape(TOKENS, NC * RANK), core_grad
```

```python
import functools

import jax
import jax.numpy as jnp
from jax import lax
from jax.experimental import pallas as pl
from jax.experimental.pallas import tpu as pltpu
from jax.sharding import Mesh
from jax.sharding import PartitionSpec as P

E = 4
RANK = 2
NR = 8
NC = 8
KC = 64
HIGH = lax.Precision.HIGHEST
F32 = jnp.float32
BF16 = jnp.bfloat16

SCORE, ROW_HIGH, ROW_LOW, OUTER, OUTER_REST = 0, 1, 2, 16, 20
RECORD = 64


def local_weights(grads, values, expand_weight, row_factors, col_factors, core, pair_index, counts):
    nmem = lax.axis_size("mem")
    tokens = grads.shape[0]
    width = values.shape[1]
    vrows = values.shape[0]
    rows = pair_index.shape[1]
    cap = rows // nmem
    high = lax.Precision.HIGHEST
    expanded = jnp.einsum(
        "tn,evn->tev",
        grads,
        lax.all_gather(expand_weight, "mem", axis=2, tiled=True),
        preferred_element_type=jnp.float32,
    ).astype(jnp.bfloat16)
    code = pair_index[0]
    local_row = pair_index[1]
    within = jnp.tile(jnp.arange(cap, dtype=jnp.int32), nmem)
    owner = jnp.repeat(jnp.arange(nmem, dtype=jnp.int32), cap)
    live = within < counts[owner]
    token = code // (NR * NC)
    row_cand = code // NC % NR
    col_cand = code % NC
    a_p = row_factors.reshape(tokens, NR, RANK)[token, row_cand]
    b_p = col_factors.reshape(tokens, NC, RANK)[token, col_cand]
    core_b = jnp.dot(b_p, core.T, precision=high)
    core_a = jnp.dot(a_p, core, precision=high)
    score = jnp.where(live, jnp.sum(a_p * core_b, -1), 0.0).astype(jnp.bfloat16)
    proj = local_row % KC % E
    pair_grad = jnp.where(live[:, None], expanded[token, proj], jnp.zeros((), jnp.bfloat16))
    got_row = lax.all_to_all(
        local_row.reshape(nmem, cap), "mem", split_axis=0, concat_axis=0, tiled=True
    ).reshape(rows)
    fetched = lax.all_to_all(
        values[got_row].reshape(nmem, cap, width), "mem", split_axis=0, concat_axis=0, tiled=True
    ).reshape(rows, width)
    own_contrib = (score.astype(jnp.float32)[:, None] * pair_grad.astype(jnp.float32)).astype(
        jnp.bfloat16
    )
    contrib = lax.all_to_all(
        own_contrib.reshape(nmem, cap, width), "mem", split_axis=0, concat_axis=0, tiled=True
    ).reshape(rows, width)
    dscore = jnp.einsum("pv,pv->p", pair_grad, fetched, preferred_element_type=jnp.float32)
    block = min(2048, rows)

    def add_block(step, total):
        onehot = (jnp.arange(vrows, dtype=jnp.int32)[:, None] == got_row[None, :]).astype(
            jnp.bfloat16
        )
        return total + jnp.dot(onehot, contrib, preferred_element_type=jnp.float32)

    value_grad = lax.fori_loop(0, rows // block, add_block, jnp.zeros((vrows, width), jnp.float32))
    dscore = lax.psum(dscore, "col")
    row_grad = jax.ops.segment_sum(
        dscore[:, None] * core_b, token * NR + row_cand, num_segments=tokens * NR
    )
    col_grad = jax.ops.segment_sum(
        dscore[:, None] * core_a, token * NC + col_cand, num_segments=tokens * NC
    )
    row_grad = row_grad.reshape(tokens, NR * RANK)
    col_grad = col_grad.reshape(tokens, NC * RANK)
    core_part = jnp.dot((dscore[:, None] * a_p).T, b_p, precision=high)
    core_grad = lax.psum(core_part, "mem")
    return (value_grad, row_grad, col_grad, core_grad)


def iota(shape, dim):
    return lax.broadcasted_iota(jnp.int32, shape, dim)


def dot_nt(x, y, precision=None):
    return lax.dot_general(
        x, y, (((1,), (1,)), ((), ())), precision=precision, preferred_element_type=F32
    )


def prepare_kernel(far, pair, counts, core, row_fac, col_fac, grads, send, scaled, hits):
    nmem = 2 * far
    rows = pair.shape[1]
    cap = rows // nmem
    half = cap // 2
    tokens, depth = grads.shape
    shard = depth // nmem
    code = pair[0:1, :]
    local_row = pair[1:2, :]
    lane = iota((1, rows), 1)
    owner = lane // cap
    limit = jnp.zeros((1, rows), jnp.int32)
    for o in range(nmem):
        limit = jnp.where(owner == o, counts[o], limit)
    live = lane % cap < limit
    token = code // (NR * NC)
    row_cand = code // NC % NR
    col_cand = code % NC
    hit = iota((tokens, rows), 0) == token
    hits[...] = jnp.where(hit, 1.0, 0.0).astype(BF16)
    factors = jnp.concatenate([row_fac[...], col_fac[...]], axis=0)
    found = jnp.dot(factors, jnp.where(hit, 1.0, 0.0), precision=HIGH, preferred_element_type=F32)
    at = iota(found.shape, 0)
    split = NR * RANK

    def pick(place):
        return jnp.sum(jnp.where(at == place, found, 0.0), axis=0, keepdims=True)

    a0, a1 = pick(row_cand * RANK), pick(row_cand * RANK + 1)
    b0, b1 = pick(split + col_cand * RANK), pick(split + col_cand * RANK + 1)
    c00, c01, c10, c11 = core[0, 0], core[0, 1], core[1, 0], core[1, 1]
    core_b0, core_b1 = c00 * b0 + c01 * b1, c10 * b0 + c11 * b1
    core_a0, core_a1 = c00 * a0 + c10 * a1, c01 * a0 + c11 * a1
    score = jnp.where(live, a0 * core_b0 + a1 * core_b1, 0.0)
    even = at % RANK == 0
    of_row = jnp.where(at // RANK == row_cand, jnp.where(even, core_b0, core_b1), 0.0)
    of_col = jnp.where((at - split) // RANK == col_cand, jnp.where(even, core_a0, core_a1), 0.0)
    scaled[...] = jnp.where(at < split, of_row, of_col)

    field = iota((2 * RECORD, rows), 0) % RECORD
    record = jnp.where(field == SCORE, score, 0.0)
    record = jnp.where(field == ROW_HIGH, (local_row // KC).astype(F32), record)
    record = jnp.where(field == ROW_LOW, (local_row % KC).astype(F32), record)
    for k, outer in enumerate((a0 * b0, a0 * b1, a1 * b0, a1 * b1)):
        top = outer.astype(BF16).astype(F32)
        record = jnp.where(field == OUTER + k, top, record)
        record = jnp.where(field == OUTER_REST + k, outer - top, record)
    record = record.astype(BF16)

    mine = rows // 2
    part = mine // 2
    q = iota((mine, rows), 0)
    base = (q % part // half * 2 + q // part) * cap + q % half
    pair_lane = iota((mine, rows), 1)

    def order(which):
        return jnp.where(pair_lane == base + which * half, 1.0, 0.0).astype(BF16)

    first, second = dot_nt(order(0), record), dot_nt(order(1), record)
    records = jnp.where(iota(first.shape, 1) < RECORD, first, second).astype(BF16)
    live_hits = jnp.where(jnp.logical_and(hit, live), 1.0, 0.0).astype(BF16)
    chosen = dot_nt(order(lax.axis_index("col")), live_hits).astype(BF16)
    taken = jnp.dot(chosen, grads[...], preferred_element_type=F32).astype(BF16)
    for z in range(far):
        for x in range(2):
            d = z * 2 + x
            other = z * 2 + 1 - x
            block = taken[x * part : (x + 1) * part]
            send[d, :, 0:shard] = block[:, d * shard : (d + 1) * shard]
            send[d, :, shard : 2 * shard] = block[:, other * shard : (other + 1) * shard]
            send[d, :, 2 * shard :] = records[x * part : (x + 1) * part]


def project_kernel(far, got, own, own_col, own_near, own_both, out):
    nmem, part, wide = got.shape
    shard = own.shape[2]
    half = part // far
    pairs = nmem * part
    col = lax.axis_index("col")
    x_own = got[:, :, 0:shard].reshape(pairs, shard)
    x_near = got[:, :, shard : 2 * shard].reshape(pairs, shard)
    record = got[:, :, 2 * shard :].reshape(pairs, 2 * RECORD).astype(F32)
    low = jnp.where(iota(record.shape, 1) == col * RECORD + ROW_LOW, record, 0.0)
    proj = jnp.sum(low, axis=1, keepdims=True).astype(jnp.int32) % E
    for at, w_own, w_near in ((col, own, own_near), (1 - col, own_col, own_both)):
        total = None
        for e in range(E):
            here = dot_nt(x_own, w_own[e]) + dot_nt(x_near, w_near[e])
            total = here if total is None else jnp.where(proj == e, here, total)
        total = total.reshape(nmem, far, half, total.shape[1])
        for z in range(far):
            out[z * 2 + at] = total[:, z].reshape(nmem * half, total.shape[3]).astype(BF16)


def lookup_kernel(far, got, values, onehot, fetched, records):
    nmem, part, wide = got.shape
    half = part // far
    z = lax.axis_index("far")
    record = got[...].astype(F32).reshape(nmem, far, half, wide)
    here = record[:, 0]
    for k in range(1, far):
        here = jnp.where(z == k, record[:, k], here)
    here = here.reshape(nmem * half, wide)
    both = jnp.concatenate([here, pltpu.roll(here, wide - RECORD, 1)], axis=0)
    records[...] = both
    row = (KC * both[:, ROW_HIGH : ROW_HIGH + 1] + both[:, ROW_LOW : ROW_LOW + 1]).astype(jnp.int32)
    hot = jnp.where(iota(onehot.shape, 1) == row, 1.0, 0.0).astype(BF16)
    onehot[...] = hot
    fetched[...] = jnp.dot(hot, values[...], preferred_element_type=F32).astype(BF16)


def reduce_kernel(far, parts, fetched, records, contrib, back):
    nmem = 2 * far
    rows = fetched.shape[0]
    half = rows // nmem // 2
    sums = []
    for which in range(2):
        total = parts[which].astype(F32)
        for z in range(1, far):
            total = total + parts[z * 2 + which].astype(F32)
        sums.append(total)
    pair_grad = jnp.concatenate(sums, axis=0).astype(BF16).astype(F32)
    record = records[...]
    contrib[...] = (record[:, SCORE : SCORE + 1] * pair_grad).astype(BF16)
    dscore = jnp.sum(pair_grad * fetched[...].astype(F32), axis=1, keepdims=True)
    me = lax.axis_index("far") * 2 + lax.axis_index("near")
    q = iota(record.shape, 0)
    place = me * (2 * half) + q // (rows // 2) * half + q % half
    spread = jnp.where(iota(record.shape, 1) == place, dscore, 0.0)
    spread = spread.reshape(2, nmem, half, record.shape[1])
    spread = jnp.sum(spread[0] + spread[1], axis=1)
    outer = jnp.sum(dscore * record, axis=0, keepdims=True)
    line = iota((8, record.shape[1]), 0)
    for s in range(nmem):
        block = jnp.where(line == 0, spread[s : s + 1], jnp.where(line == 1, outer, 0.0))
        back[2 * s] = block
        back[2 * s + 1] = block


def value_kernel(onehot, contrib, out):
    out[...] = lax.dot_general(
        onehot[...], contrib[...], (((0,), (0,)), ((), ())), preferred_element_type=F32
    )


def finish_kernel(back, scaled, hits, row_out, col_out, core_out):
    total = jnp.sum(back[...], axis=0)
    dscore = total[0:1]
    outer = total[1:2]
    grads = dot_nt(scaled[...] * dscore, hits[...].astype(F32), HIGH)
    split = row_out.shape[0]
    row_out[...] = grads[:split]
    col_out[...] = grads[split:]
    lane = iota(outer.shape, 1)
    r, s = iota((RANK, RANK), 0), iota((RANK, RANK), 1)
    result = jnp.zeros((RANK, RANK), F32)
    for k in range(RANK * RANK):
        mask = jnp.logical_or(lane == OUTER + k, lane == OUTER_REST + k)
        value = jnp.sum(jnp.where(mask, outer, 0.0), axis=1, keepdims=True)
        result = jnp.where(r * RANK + s == k, value, result)
    core_out[...] = result


VMEM = pl.BlockSpec(memory_space=pltpu.VMEM)
SMEM = pl.BlockSpec(memory_space=pltpu.SMEM)


def call(kernel, name, outs, ins, flops, moved, limit=24):
    return pl.pallas_call(
        kernel,
        name=name,
        out_shape=outs,
        in_specs=ins,
        out_specs=jax.tree.map(lambda _: VMEM, outs),
        cost_estimate=pl.CostEstimate(flops=flops, bytes_accessed=moved, transcendentals=0),
        compiler_params=pltpu.CompilerParams(vmem_limit_bytes=limit << 20),
    )


def shape(dims, kind):
    return jax.ShapeDtypeStruct(dims, kind)


def local_pairs(grads, values, expand_weight, row_factors, col_factors, core, pair_index, counts):
    far = lax.axis_size("far")
    nmem = 2 * far
    tokens, depth = grads.shape
    vrows, width = values.shape
    rows = pair_index.shape[1]
    shard = depth // nmem
    swap = [(0, 1), (1, 0)]
    own_near = lax.ppermute(expand_weight, "near", swap)
    own_col = lax.ppermute(expand_weight, "col", swap)
    own_both = lax.ppermute(own_near, "col", swap)
    part = rows // 4
    wide = 2 * shard + 2 * RECORD
    send, scaled, hits = call(
        functools.partial(prepare_kernel, far),
        "prepare",
        (
            shape((nmem, part, wide), BF16),
            shape((NR * RANK + NC * RANK, rows), F32),
            shape((tokens, rows), BF16),
        ),
        [VMEM, SMEM, SMEM, VMEM, VMEM, VMEM],
        rows * tokens * depth,
        2 * tokens * depth,
    )(pair_index, counts, core, row_factors.T, col_factors.T, grads)
    got = lax.all_to_all(send, ("far", "near"), split_axis=0, concat_axis=0, tiled=True)
    parts = call(
        functools.partial(project_kernel, far),
        "project",
        shape((2 * far, rows // 2, width), BF16),
        [VMEM] * 5,
        4 * E * nmem * part * shard * width * 2,
        8 * E * width * shard,
    )(got, expand_weight, own_col, own_near, own_both)
    parts = lax.all_to_all(parts, ("far", "col"), split_axis=0, concat_axis=0, tiled=True)
    onehot, fetched, records = call(
        functools.partial(lookup_kernel, far),
        "lookup",
        (
            shape((rows, vrows), BF16),
            shape((rows, width), BF16),
            shape((rows, 2 * RECORD), F32),
        ),
        [VMEM, VMEM],
        2 * rows * vrows * width,
        2 * vrows * width,
    )(got[:, :, 2 * shard :], values)
    contrib, back = call(
        functools.partial(reduce_kernel, far),
        "reduce",
        (shape((rows, width), BF16), shape((2 * nmem, 8, 2 * RECORD), F32)),
        [VMEM] * 3,
        8 * rows * width,
        10 * rows * width,
    )(parts, fetched, records)
    back = lax.all_to_all(back, ("far", "near", "col"), split_axis=0, concat_axis=0, tiled=True)
    value_grad = call(
        value_kernel,
        "value_rows",
        shape((vrows, width), F32),
        [VMEM] * 2,
        2 * rows * vrows * width,
        4 * vrows * width,
    )(onehot, contrib)
    row_grad, col_grad, core_grad = call(
        finish_kernel,
        "finish",
        (
            shape((NR * RANK, tokens), F32),
            shape((NC * RANK, tokens), F32),
            shape((RANK, RANK), F32),
        ),
        [VMEM] * 3,
        2 * rows * tokens * 64,
        8 * rows * tokens,
    )(back, scaled, hits)
    return value_grad, row_grad.T, col_grad.T, core_grad


def solution(mesh):
    ngroup, nmem, ncol = (mesh.shape[a] for a in ("group", "mem", "col"))

    def run(*args):
        rows = args[6].shape[1] // (ngroup * nmem)
        depth = args[0].shape[1]
        fits = nmem % 2 == 0 and ncol == 2 and rows == 16 * nmem == 128
        fits = fits and depth % (128 * nmem) == 0
        if fits and nmem * rows <= E * depth:
            used = Mesh(
                mesh.devices.reshape(ngroup, nmem // 2, 2, ncol), ("group", "far", "near", "col")
            )
            mem, body = ("far", "near"), local_pairs
        else:
            used, mem, body = mesh, ("mem",), local_weights
        both = ("group",) + mem
        return jax.shard_map(
            body,
            mesh=used,
            in_specs=(
                P(both, None),
                P(mem, "col"),
                P(None, "col", mem),
                P(both, None),
                P(both, None),
                P(),
                P(None, both),
                P(both),
            ),
            out_specs=(
                P(both, "col"),
                P(both, None),
                P(both, None),
                P("group", None),
            ),
            check_vma=False,
        )(*args)

    return run
```

```python
import functools
import math

import jax
import jax.numpy as jnp
from jax import lax
from jax.experimental import pallas as pl
from jax.experimental.pallas import tpu as pltpu
from jax.sharding import Mesh
from jax.sharding import PartitionSpec as P

E = 4
RANK = 2
NR = 8
NC = 8
KC = 64
F32 = jnp.float32
BF16 = jnp.bfloat16

SCORE, ROW_HIGH, ROW_LOW, OUTER, OUTER_REST = 0, 1, 2, 4, 12
RECORD = 16
FULL = 32000.0


def local_weights(grads, values, expand_weight, row_factors, col_factors, core, pair_index, counts):
    nmem = lax.axis_size("mem")
    tokens = grads.shape[0]
    width = values.shape[1]
    vrows = values.shape[0]
    rows = pair_index.shape[1]
    cap = rows // nmem
    high = lax.Precision.HIGHEST
    expanded = jnp.einsum(
        "tn,evn->tev",
        grads,
        lax.all_gather(expand_weight, "mem", axis=2, tiled=True),
        preferred_element_type=jnp.float32,
    ).astype(jnp.bfloat16)
    code = pair_index[0]
    local_row = pair_index[1]
    within = jnp.tile(jnp.arange(cap, dtype=jnp.int32), nmem)
    owner = jnp.repeat(jnp.arange(nmem, dtype=jnp.int32), cap)
    live = within < counts[owner]
    token = code // (NR * NC)
    row_cand = code // NC % NR
    col_cand = code % NC
    a_p = row_factors.reshape(tokens, NR, RANK)[token, row_cand]
    b_p = col_factors.reshape(tokens, NC, RANK)[token, col_cand]
    core_b = jnp.dot(b_p, core.T, precision=high)
    core_a = jnp.dot(a_p, core, precision=high)
    score = jnp.where(live, jnp.sum(a_p * core_b, -1), 0.0).astype(jnp.bfloat16)
    proj = local_row % KC % E
    pair_grad = jnp.where(live[:, None], expanded[token, proj], jnp.zeros((), jnp.bfloat16))
    got_row = lax.all_to_all(
        local_row.reshape(nmem, cap), "mem", split_axis=0, concat_axis=0, tiled=True
    ).reshape(rows)
    fetched = lax.all_to_all(
        values[got_row].reshape(nmem, cap, width), "mem", split_axis=0, concat_axis=0, tiled=True
    ).reshape(rows, width)
    own_contrib = (score.astype(jnp.float32)[:, None] * pair_grad.astype(jnp.float32)).astype(
        jnp.bfloat16
    )
    contrib = lax.all_to_all(
        own_contrib.reshape(nmem, cap, width), "mem", split_axis=0, concat_axis=0, tiled=True
    ).reshape(rows, width)
    dscore = jnp.einsum("pv,pv->p", pair_grad, fetched, preferred_element_type=jnp.float32)
    block = min(2048, rows)

    def add_block(step, total):
        onehot = (jnp.arange(vrows, dtype=jnp.int32)[:, None] == got_row[None, :]).astype(
            jnp.bfloat16
        )
        return total + jnp.dot(onehot, contrib, preferred_element_type=jnp.float32)

    value_grad = lax.fori_loop(0, rows // block, add_block, jnp.zeros((vrows, width), jnp.float32))
    dscore = lax.psum(dscore, "col")
    row_grad = jax.ops.segment_sum(
        dscore[:, None] * core_b, token * NR + row_cand, num_segments=tokens * NR
    )
    col_grad = jax.ops.segment_sum(
        dscore[:, None] * core_a, token * NC + col_cand, num_segments=tokens * NC
    )
    row_grad = row_grad.reshape(tokens, NR * RANK)
    col_grad = col_grad.reshape(tokens, NC * RANK)
    core_part = jnp.dot((dscore[:, None] * a_p).T, b_p, precision=high)
    core_grad = lax.psum(core_part, "mem")
    return (value_grad, row_grad, col_grad, core_grad)


def iota(shape, dim):
    return lax.broadcasted_iota(jnp.int32, shape, dim)


def dot_nn(x, y):
    return jnp.dot(x, y, preferred_element_type=F32)


def dot_nt(x, y):
    return lax.dot_general(x, y, (((1,), (1,)), ((), ())), preferred_element_type=F32)


def thirds(x):
    first = x.astype(BF16)
    rest = x - first.astype(F32)
    second = rest.astype(BF16)
    third = (rest - second.astype(F32)).astype(BF16)
    return jnp.concatenate([first, second, third], axis=0)


def add_thirds(y):
    n = y.shape[0] // 3
    return (y[2 * n :] + y[n : 2 * n]) + y[:n]


def place():
    return lax.axis_index("far"), lax.axis_index("near"), lax.axis_index("col")


def prepare_kernel(
    far, pair_hbm, counts_hbm, core_hbm, row_hbm, col_hbm, grads_hbm, *refs
):
    sends, (scaled, hits), (pair, counts, core, row_fac, col_fac, grads, sems) = (
        refs[:far],
        refs[far : far + 2],
        refs[far + 2 :],
    )
    sources = (pair_hbm, counts_hbm, core_hbm, row_hbm, col_hbm, grads_hbm)
    targets = (pair, counts, core, row_fac, col_fac, grads)
    copies = [
        pltpu.make_async_copy(source, target, sems.at[k])
        for k, (source, target) in enumerate(zip(sources, targets))
    ]
    for copy in copies:
        copy.start()
    for copy in copies[:-1]:
        copy.wait()
    z, x, c = place()
    nmem = 2 * far
    rows = pair.shape[1]
    cap = rows // nmem
    half = cap // 2
    tokens, depth = grads.shape
    shard = depth // nmem
    code = pair[0:1, :]
    local_row = pair[1:2, :]
    lane = iota((1, rows), 1)
    owner = lane // cap
    limit = jnp.zeros((1, rows), jnp.int32)
    for o in range(nmem):
        limit = jnp.where(owner == o, counts[0:1, o : o + 1], limit)
    live = lane % cap < limit
    token = code // (NR * NC)
    row_cand = code // NC % NR
    col_cand = code % NC
    hit = iota((tokens, rows), 0) == token
    hot = jnp.where(hit, 1.0, 0.0).astype(BF16)
    hits[...] = hot
    factors = jnp.concatenate([row_fac[...], col_fac[...]], axis=0)
    found = add_thirds(dot_nn(thirds(factors), hot))
    at = iota(found.shape, 0)
    split = NR * RANK

    def pick(row):
        return jnp.sum(jnp.where(at == row, found, 0.0), axis=0, keepdims=True)

    a0, a1 = pick(row_cand * RANK), pick(row_cand * RANK + 1)
    b0, b1 = pick(split + col_cand * RANK), pick(split + col_cand * RANK + 1)
    c00, c01, c10, c11 = core[0:1, 0:1], core[0:1, 1:2], core[1:2, 0:1], core[1:2, 1:2]
    core_b0, core_b1 = c00 * b0 + c01 * b1, c10 * b0 + c11 * b1
    core_a0, core_a1 = c00 * a0 + c10 * a1, c01 * a0 + c11 * a1
    score = jnp.where(live, a0 * core_b0 + a1 * core_b1, 0.0)
    even = at % RANK == 0
    of_row = jnp.where(at // RANK == row_cand, jnp.where(even, core_b0, core_b1), 0.0)
    of_col = jnp.where((at - split) // RANK == col_cand, jnp.where(even, core_a0, core_a1), 0.0)
    scaled[...] = jnp.where(at < split, of_row, of_col)

    field = iota((RECORD, rows), 0)
    record = jnp.where(field == SCORE, score, 0.0)
    record = jnp.where(field == ROW_HIGH, (local_row // KC).astype(F32), record)
    record = jnp.where(field == ROW_LOW, (local_row % KC).astype(F32), record)
    for k, outer in enumerate((a0 * b0, a0 * b1, a1 * b0, a1 * b1)):
        top = outer.astype(BF16).astype(F32)
        record = jnp.where(field == OUTER + k, top, record)
        record = jnp.where(field == OUTER_REST + k, outer - top, record)

    to = iota((rows, rows), 1)
    to_m, to_y = to // (2 * cap), to // cap % 2
    to_pair = ((to_m ^ z) * 2 + (to_y ^ x)) * cap + (to // half % 2 ^ c) * half + to % half
    order = jnp.where(iota((rows, rows), 0) == to_pair, 1.0, 0.0).astype(BF16)
    records = dot_nn(record.astype(BF16), order).astype(BF16)

    mine = rows // 2
    q = iota((mine, rows), 0)
    q_pair = ((q // cap ^ z) * 2 + (q // half % 2 ^ x)) * cap + c * half + q % half
    take = jnp.where(iota((mine, rows), 1) == q_pair, 1.0, 0.0).astype(BF16)
    live_hits = jnp.where(jnp.logical_and(hit, live), 1.0, 0.0).astype(BF16)
    chosen = dot_nt(take, live_hits).astype(BF16)
    copies[-1].wait()
    for k in range(far):
        blocks = []
        for y in range(2):
            start = pl.multiple_of(((z ^ k) * 2 + (x ^ y)) * shard, shard)
            taken = dot_nn(chosen, grads[:, pl.ds(start, shard)]).astype(BF16)
            blocks += [taken[:, :128], taken[:, 128:]]
        sends[k][...] = jnp.concatenate(blocks + [records], axis=0)


def project_kernel(far, *refs):
    ours, theirs = refs[:far], refs[far : 2 * far]
    own, near = refs[2 * far : 2 * far + 2]
    whole, coded = refs[2 * far + 2], refs[2 * far + 3 :]
    mine = (ours[0].shape[0] - RECORD) // 4
    cap = mine // far // 2 * 2
    half = cap // 2
    rows = 2 * mine
    lane, line = iota((rows, rows), 1), iota((rows, rows), 0)
    mask = line % mine // half * cap + line // mine * half + line % half == lane
    firsts, seconds, projs = [], [], []
    for k in range(far):
        for block in (ours[k], theirs[k]):
            firsts.append(jnp.concatenate([block[0:mine], block[mine : 2 * mine]], axis=1))
            seconds.append(
                jnp.concatenate([block[2 * mine : 3 * mine], block[3 * mine : 4 * mine]], axis=1)
            )
        record = ours[k][4 * mine : 4 * mine + RECORD].astype(F32)
        low = jnp.where(mask, record[ROW_LOW : ROW_LOW + 1], 0.0)
        projs.append(jnp.sum(low, axis=1, keepdims=True))
    first, second = jnp.concatenate(firsts, axis=0), jnp.concatenate(seconds, axis=0)
    proj = jnp.concatenate(projs, axis=0).astype(jnp.int32) % E
    total = None
    for e in range(E):
        here = dot_nt(first, own[e]) + dot_nt(second, near[e])
        total = here if total is None else jnp.where(proj == e, here, total)

    def rows_for(j):
        pieces = []
        for y in range(2):
            for n in range(far):
                for g in range(2):
                    start = (j ^ n) * rows + g * mine + n * cap + y * half
                    pieces.append(total[start : start + half])
        return jnp.concatenate(pieces, axis=0)

    whole[...] = rows_for(0)
    diagonal = line == lane
    for j in range(1, far):
        part = rows_for(j)
        top = jnp.max(jnp.abs(part), axis=1, keepdims=True)
        power = jnp.floor(jnp.log(jnp.maximum(top, 2.0**-100)) * (1 / math.log(2))) + 1.0
        level = jnp.abs(part) * jnp.exp2(-power)
        root = level * lax.rsqrt(jnp.maximum(level, 1e-30)) * FULL
        code = jnp.floor(jnp.where(part < 0, -root, root) + 0.5)
        powers = jnp.sum(jnp.where(diagonal, power, 0.0), axis=0, keepdims=True)
        powers = jnp.broadcast_to(powers, (RECORD, rows))
        block = jnp.concatenate([code[:, :128], code[:, 128:], powers], axis=0)
        coded[j - 1][...] = block.astype(jnp.int32).astype(jnp.int16)


def lookup_kernel(far, *refs):
    blocks, (values, near_values), (fetched, records, value_rows) = (
        refs[:far],
        refs[far : far + 2],
        refs[far + 2 :],
    )
    rows = records.shape[0]
    group = rows // far
    lane, line = iota((rows, rows), 1), iota((rows, rows), 0)
    total = jnp.zeros((RECORD, rows), F32)
    for n in range(far):
        tile = blocks[n][2 * rows : 2 * rows + RECORD]
        source = n * group + lane // (rows // 2) * (group // 2) + lane % (group // 2)
        inside = lane // (group // 2) % far == n
        move = jnp.where(jnp.logical_and(line == source, inside), 1.0, 0.0).astype(BF16)
        total = total + dot_nn(tile, move)
    value_row = KC * total[ROW_HIGH : ROW_HIGH + 1] + total[ROW_LOW : ROW_LOW + 1]
    value_rows[...] = jnp.broadcast_to(value_row, value_rows.shape)
    padded = jnp.concatenate([total, jnp.zeros((rows - RECORD, rows), F32)], axis=0).astype(BF16)
    column = dot_nt(jnp.where(line == lane, 1.0, 0.0).astype(BF16), padded)
    records[...] = column
    row = KC * column[:, ROW_HIGH : ROW_HIGH + 1] + column[:, ROW_LOW : ROW_LOW + 1]
    hot = iota((rows, values.shape[0]), 1) == row.astype(jnp.int32)
    hot = jnp.where(hot, 1.0, 0.0).astype(BF16)
    fetched[: rows // 2] = dot_nn(hot[: rows // 2], values[...])
    fetched[rows // 2 :] = dot_nn(hot[rows // 2 :], near_values[...])


def reduce_kernel(far, *refs):
    (whole, fetched, records, value_rows), coded, (contrib, pass_on, back) = (
        refs[:4],
        refs[4 : 3 + far],
        refs[3 + far :],
    )
    z, x, c = place()
    rows, width = whole.shape
    half = rows // far // 4
    line, lane = iota((rows, rows), 0), iota((rows, rows), 1)
    diagonal = line == lane
    total = whole[...]
    for block in coded:
        code = block[...].astype(jnp.int32).astype(F32)
        power = jnp.where(diagonal, code[2 * rows : 2 * rows + 1], 0.0)
        scale = jnp.exp2(jnp.sum(power, axis=1, keepdims=True)) * (1 / FULL**2)
        value = jnp.concatenate([code[:rows], code[rows : 2 * rows]], axis=1)
        total = total + value * jnp.abs(value) * scale
    pair_grad = total.astype(BF16).astype(F32)
    record = records[...]
    share = record[:, SCORE : SCORE + 1] * pair_grad
    contrib[...] = share[: rows // 2].astype(BF16)
    send = value_rows[0:1]
    send_high = jnp.floor(send * (1 / KC))
    tile = iota((RECORD, width), 0)
    spare = jnp.zeros((1, width - rows), F32)
    high_row = jnp.concatenate([send_high, spare], axis=1)
    low_row = jnp.concatenate([send - KC * send_high, spare], axis=1)
    tail = jnp.where(tile == 0, high_row, jnp.where(tile == 1, low_row, 0.0))
    pass_on[...] = jnp.concatenate([share[rows // 2 :], tail], axis=0).astype(BF16)
    dscore = jnp.sum(pair_grad * fetched[...], axis=1, keepdims=True)
    owner = z * 2 + (line // (rows // 2) ^ x)
    target = owner * (2 * half) + (line // half % 2 ^ c) * half + line % half
    spread = jnp.where(lane == target, dscore, 0.0).reshape(2, far, 2 * half, rows)
    spread = jnp.sum(spread[0] + spread[1], axis=1)
    outer = jnp.sum(dscore * record, axis=0, keepdims=True)
    empty = jnp.zeros((7 - far, rows), F32)
    block = jnp.concatenate([spread, outer, empty], axis=0)
    for k in range(back.shape[0]):
        back[k] = block


def value_kernel(contrib, passed, value_rows, out):
    half = contrib.shape[0]
    rows = 2 * half
    tail = passed[half : half + RECORD].astype(F32)
    lane = iota((1, rows), 1)
    other = (KC * tail[0:1] + tail[1:2])[:, :rows]
    row = jnp.where(lane < half, value_rows[0:1], other).astype(jnp.int32)
    hot = jnp.where(iota((out.shape[0], rows), 0) == row, 1.0, 0.0).astype(BF16)
    out[...] = dot_nn(hot, jnp.concatenate([contrib[...], passed[:half]], axis=0))


def finish_kernel(far, back, scaled, hits, row_out, col_out, core_out):
    z, x, _ = place()
    line = iota(back.shape[1:], 0)
    total = jnp.zeros(back.shape[1:], F32)
    for k in range(back.shape[0]):
        mine = jnp.logical_and(line == (k // 4 ^ z), k // 2 % 2 == x)
        total = total + jnp.where(jnp.logical_or(mine, line == far), back[k], 0.0)
    dscore = jnp.sum(total[:far], axis=0, keepdims=True)
    outer = total[far : far + 1]
    grads = add_thirds(dot_nt(thirds(scaled[...] * dscore), hits[...]))
    split = row_out.shape[0]
    row_out[...] = grads[:split]
    col_out[...] = grads[split:]
    lane = iota(outer.shape, 1)
    r, s = iota((RANK, RANK), 0), iota((RANK, RANK), 1)
    result = jnp.zeros((RANK, RANK), F32)
    for k in range(RANK * RANK):
        mask = jnp.logical_or(lane == OUTER + k, lane == OUTER_REST + k)
        value = jnp.sum(jnp.where(mask, outer, 0.0), axis=1, keepdims=True)
        result = jnp.where(r * RANK + s == k, value, result)
    core_out[...] = result


VMEM = pl.BlockSpec(memory_space=pltpu.VMEM)
HBM = pl.BlockSpec(memory_space=pl.ANY)


def call(kernel, name, outs, ins, flops, moved, scratch=(), limit=24):
    return pl.pallas_call(
        kernel,
        name=name,
        out_shape=outs,
        in_specs=ins,
        out_specs=jax.tree.map(lambda _: VMEM, outs),
        scratch_shapes=scratch,
        cost_estimate=pl.CostEstimate(flops=flops, bytes_accessed=moved, transcendentals=0),
        compiler_params=pltpu.CompilerParams(vmem_limit_bytes=limit << 20),
    )


def shape(dims, kind):
    return jax.ShapeDtypeStruct(dims, kind)


def local_pairs(grads, values, expand_weight, row_factors, col_factors, core, pair_index, counts):
    far = lax.axis_size("far")
    nmem = 2 * far
    tokens, depth = grads.shape
    vrows, width = values.shape
    rows = pair_index.shape[1]
    factors = NR * RANK + NC * RANK
    swap = [(0, 1), (1, 0)]

    def along_far(block, k):
        return lax.ppermute(block, "far", [(i, i ^ k) for i in range(far)])

    near_weight = lax.ppermute(expand_weight, "near", swap)
    block = shape((2 * rows + RECORD, 128), BF16)
    *sends, scaled, hits = call(
        functools.partial(prepare_kernel, far),
        "prepare",
        (block,) * far + (shape((factors, rows), F32), shape((tokens, rows), BF16)),
        [HBM] * 6,
        rows * tokens * depth,
        2 * tokens * depth,
        (
            pltpu.VMEM((2, rows), jnp.int32),
            pltpu.VMEM((1, nmem), jnp.int32),
            pltpu.VMEM((RANK, RANK), F32),
            pltpu.VMEM((NR * RANK, tokens), F32),
            pltpu.VMEM((NC * RANK, tokens), F32),
            pltpu.VMEM((tokens, depth), BF16),
            pltpu.SemaphoreType.DMA((6,)),
        ),
    )(pair_index, counts.reshape(1, nmem), core, row_factors.T, col_factors.T, grads)
    ours = [sends[0]] + [along_far(sends[k], k) for k in range(1, far)]
    theirs = [lax.ppermute(got, "col", swap) for got in ours]
    near_values = lax.ppermute(values, "near", swap)
    code = shape((2 * rows + RECORD, 128), jnp.int16)
    whole, *coded = call(
        functools.partial(project_kernel, far),
        "project",
        (shape((rows, width), F32),) + (code,) * (far - 1),
        [VMEM] * (2 * far + 2),
        4 * E * far * rows * depth // far * width,
        8 * E * width * depth // nmem,
    )(*ours, *theirs, expand_weight, near_weight)
    coded = [along_far(coded[j - 1], j) for j in range(1, far)]
    fetched, records, value_rows = call(
        functools.partial(lookup_kernel, far),
        "lookup",
        (shape((rows, width), F32), shape((rows, rows), F32), shape((8, rows), F32)),
        [VMEM] * (far + 2),
        2 * rows * vrows * width,
        4 * vrows * width,
    )(*ours, values, near_values)
    contrib, pass_on, back = call(
        functools.partial(reduce_kernel, far),
        "reduce",
        (
            shape((rows // 2, width), BF16),
            shape((rows // 2 + RECORD, width), BF16),
            shape((2 * nmem, 8, rows), F32),
        ),
        [VMEM] * (3 + far),
        8 * rows * width,
        10 * rows * width,
    )(whole, fetched, records, value_rows, *coded)
    back = lax.all_to_all(back, ("far", "near", "col"), split_axis=0, concat_axis=0, tiled=True)
    passed = lax.ppermute(pass_on, "near", swap)
    value_grad = call(
        value_kernel,
        "value_rows",
        shape((vrows, width), F32),
        [VMEM] * 3,
        2 * rows * vrows * width,
        4 * vrows * width,
    )(contrib, passed, value_rows)
    row_grad, col_grad, core_grad = call(
        functools.partial(finish_kernel, far),
        "finish",
        (
            shape((NR * RANK, tokens), F32),
            shape((NC * RANK, tokens), F32),
            shape((RANK, RANK), F32),
        ),
        [VMEM] * 3,
        2 * rows * tokens * 96,
        4 * rows * tokens,
    )(back, scaled, hits)
    return value_grad, row_grad.T, col_grad.T, core_grad


def solution(mesh):
    ngroup, nmem, ncol = (mesh.shape[a] for a in ("group", "mem", "col"))

    def run(*args):
        rows = args[6].shape[1] // (ngroup * nmem)
        depth = args[0].shape[1]
        fits = nmem % 2 == 0 and ncol == 2 and rows == 16 * nmem == 128
        fits = fits and depth == 256 * nmem and args[1].shape[1] == 256 * ncol
        if fits and nmem * rows <= E * depth:
            used = Mesh(
                mesh.devices.reshape(ngroup, nmem // 2, 2, ncol), ("group", "far", "near", "col")
            )
            mem, body = ("far", "near"), local_pairs
        else:
            used, mem, body = mesh, ("mem",), local_weights
        both = ("group",) + mem
        return jax.shard_map(
            body,
            mesh=used,
            in_specs=(
                P(both, None),
                P(mem, "col"),
                P(None, "col", mem),
                P(both, None),
                P(both, None),
                P(),
                P(None, both),
                P(both),
            ),
            out_specs=(
                P(both, "col"),
                P(both, None),
                P(both, None),
                P("group", None),
            ),
            check_vma=False,
        )(*args)

    return run
```

```python
import functools
import math

import jax
import jax.numpy as jnp
from jax import lax
from jax.experimental import pallas as pl
from jax.experimental.pallas import tpu as pltpu
from jax.sharding import Mesh
from jax.sharding import PartitionSpec as P

E = 4
RANK = 2
NR = 8
NC = 8
KC = 64
F32 = jnp.float32
BF16 = jnp.bfloat16

SCORE, ROW_HIGH, ROW_LOW, OUTER, OUTER_REST = 0, 1, 2, 4, 12
RECORD = 16
FULL = 32000.0
WHOLE = 2


def local_weights(grads, values, expand_weight, row_factors, col_factors, core, pair_index, counts):
    nmem = lax.axis_size("mem")
    tokens = grads.shape[0]
    width = values.shape[1]
    vrows = values.shape[0]
    rows = pair_index.shape[1]
    cap = rows // nmem
    high = lax.Precision.HIGHEST
    expanded = jnp.einsum(
        "tn,evn->tev",
        grads,
        lax.all_gather(expand_weight, "mem", axis=2, tiled=True),
        preferred_element_type=jnp.float32,
    ).astype(jnp.bfloat16)
    code = pair_index[0]
    local_row = pair_index[1]
    within = jnp.tile(jnp.arange(cap, dtype=jnp.int32), nmem)
    owner = jnp.repeat(jnp.arange(nmem, dtype=jnp.int32), cap)
    live = within < counts[owner]
    token = code // (NR * NC)
    row_cand = code // NC % NR
    col_cand = code % NC
    a_p = row_factors.reshape(tokens, NR, RANK)[token, row_cand]
    b_p = col_factors.reshape(tokens, NC, RANK)[token, col_cand]
    core_b = jnp.dot(b_p, core.T, precision=high)
    core_a = jnp.dot(a_p, core, precision=high)
    score = jnp.where(live, jnp.sum(a_p * core_b, -1), 0.0).astype(jnp.bfloat16)
    proj = local_row % KC % E
    pair_grad = jnp.where(live[:, None], expanded[token, proj], jnp.zeros((), jnp.bfloat16))
    got_row = lax.all_to_all(
        local_row.reshape(nmem, cap), "mem", split_axis=0, concat_axis=0, tiled=True
    ).reshape(rows)
    fetched = lax.all_to_all(
        values[got_row].reshape(nmem, cap, width), "mem", split_axis=0, concat_axis=0, tiled=True
    ).reshape(rows, width)
    own_contrib = (score.astype(jnp.float32)[:, None] * pair_grad.astype(jnp.float32)).astype(
        jnp.bfloat16
    )
    contrib = lax.all_to_all(
        own_contrib.reshape(nmem, cap, width), "mem", split_axis=0, concat_axis=0, tiled=True
    ).reshape(rows, width)
    dscore = jnp.einsum("pv,pv->p", pair_grad, fetched, preferred_element_type=jnp.float32)
    block = min(2048, rows)

    def add_block(step, total):
        onehot = (jnp.arange(vrows, dtype=jnp.int32)[:, None] == got_row[None, :]).astype(
            jnp.bfloat16
        )
        return total + jnp.dot(onehot, contrib, preferred_element_type=jnp.float32)

    value_grad = lax.fori_loop(0, rows // block, add_block, jnp.zeros((vrows, width), jnp.float32))
    dscore = lax.psum(dscore, "col")
    row_grad = jax.ops.segment_sum(
        dscore[:, None] * core_b, token * NR + row_cand, num_segments=tokens * NR
    )
    col_grad = jax.ops.segment_sum(
        dscore[:, None] * core_a, token * NC + col_cand, num_segments=tokens * NC
    )
    row_grad = row_grad.reshape(tokens, NR * RANK)
    col_grad = col_grad.reshape(tokens, NC * RANK)
    core_part = jnp.dot((dscore[:, None] * a_p).T, b_p, precision=high)
    core_grad = lax.psum(core_part, "mem")
    return (value_grad, row_grad, col_grad, core_grad)


def iota(shape, dim):
    return lax.broadcasted_iota(jnp.int32, shape, dim)


def dot_nn(x, y):
    return jnp.dot(x, y, preferred_element_type=F32)


def dot_nt(x, y):
    return lax.dot_general(x, y, (((1,), (1,)), ((), ())), preferred_element_type=F32)


def thirds(x):
    first = x.astype(BF16)
    rest = x - first.astype(F32)
    second = rest.astype(BF16)
    third = (rest - second.astype(F32)).astype(BF16)
    return jnp.concatenate([first, second, third], axis=0)


def add_thirds(y):
    n = y.shape[0] // 3
    return (y[2 * n :] + y[n : 2 * n]) + y[:n]


def place():
    return lax.axis_index("far"), lax.axis_index("near"), lax.axis_index("col")


def prepare_kernel(far, first, last, extra, *refs):
    sources, refs = refs[:6], refs[6:]
    sends, refs = refs[: last - first], refs[last - first :]
    if extra:
        (scaled, hits), refs = refs[:2], refs[2:]
    targets, sems = refs[:6], refs[6]
    pair, counts, core, row_fac, col_fac, grads = targets
    copies = [
        pltpu.make_async_copy(source, target, sems.at[k])
        for k, (source, target) in enumerate(zip(sources, targets))
    ]
    for copy in copies:
        copy.start()
    for copy in copies[:-1]:
        copy.wait()
    z, x, c = place()
    nmem = 2 * far
    rows = pair.shape[1]
    cap = rows // nmem
    half = cap // 2
    tokens, depth = grads.shape
    shard = depth // nmem
    code = pair[0:1, :]
    local_row = pair[1:2, :]
    lane = iota((1, rows), 1)
    owner = lane // cap
    limit = jnp.zeros((1, rows), jnp.int32)
    for o in range(nmem):
        limit = jnp.where(owner == o, counts[0:1, o : o + 1], limit)
    live = lane % cap < limit
    token = code // (NR * NC)
    row_cand = code // NC % NR
    col_cand = code % NC
    hit = iota((tokens, rows), 0) == token
    hot = jnp.where(hit, 1.0, 0.0).astype(BF16)
    factors = jnp.concatenate([row_fac[...], col_fac[...]], axis=0)
    found = add_thirds(dot_nn(thirds(factors), hot))
    at = iota(found.shape, 0)
    split = NR * RANK

    def pick(row):
        return jnp.sum(jnp.where(at == row, found, 0.0), axis=0, keepdims=True)

    a0, a1 = pick(row_cand * RANK), pick(row_cand * RANK + 1)
    b0, b1 = pick(split + col_cand * RANK), pick(split + col_cand * RANK + 1)
    c00, c01, c10, c11 = core[0:1, 0:1], core[0:1, 1:2], core[1:2, 0:1], core[1:2, 1:2]
    core_b0, core_b1 = c00 * b0 + c01 * b1, c10 * b0 + c11 * b1
    score = jnp.where(live, a0 * core_b0 + a1 * core_b1, 0.0)
    if extra:
        hits[...] = hot
        core_a0, core_a1 = c00 * a0 + c10 * a1, c01 * a0 + c11 * a1
        even = at % RANK == 0
        of_row = jnp.where(at // RANK == row_cand, jnp.where(even, core_b0, core_b1), 0.0)
        of_col = jnp.where((at - split) // RANK == col_cand, jnp.where(even, core_a0, core_a1), 0.0)
        scaled[...] = jnp.where(at < split, of_row, of_col)

    field = iota((RECORD, rows), 0)
    record = jnp.where(field == SCORE, score, 0.0)
    record = jnp.where(field == ROW_HIGH, (local_row // KC).astype(F32), record)
    record = jnp.where(field == ROW_LOW, (local_row % KC).astype(F32), record)
    for k, outer in enumerate((a0 * b0, a0 * b1, a1 * b0, a1 * b1)):
        top = outer.astype(BF16).astype(F32)
        record = jnp.where(field == OUTER + k, top, record)
        record = jnp.where(field == OUTER_REST + k, outer - top, record)

    to = iota((rows, rows), 1)
    to_m, to_y = to // (2 * cap), to // cap % 2
    to_pair = ((to_m ^ z) * 2 + (to_y ^ x)) * cap + (to // half % 2 ^ c) * half + to % half
    order = jnp.where(iota((rows, rows), 0) == to_pair, 1.0, 0.0).astype(BF16)
    records = dot_nn(record.astype(BF16), order).astype(BF16)

    q = iota((rows, rows), 0)
    mine = rows // 2
    q_pair = ((q % mine // cap ^ z) * 2 + (q // half % 2 ^ x)) * cap
    q_pair = q_pair + (q // mine ^ c) * half + q % half
    take = jnp.where(iota((rows, rows), 1) == q_pair, 1.0, 0.0).astype(BF16)
    live_hits = jnp.where(jnp.logical_and(hit, live), 1.0, 0.0).astype(BF16)
    chosen = dot_nt(take, live_hits).astype(BF16)
    copies[-1].wait()
    for k in range(first, last):
        taken = []
        for y in range(2):
            start = pl.multiple_of(((z ^ k) * 2 + (x ^ y)) * shard, shard)
            part = grads[:, pl.ds(start, shard)]
            taken.append(dot_nn(chosen if k < WHOLE else chosen[:mine], part).astype(BF16))
        blocks = []
        for g in range(2 if k < WHOLE else 1):
            for part in taken:
                part = part[g * mine : (g + 1) * mine]
                blocks += [part[:, :128], part[:, 128:]]
        sends[k - first][...] = jnp.concatenate(blocks + [records], axis=0)


def project_kernel(far, *refs):
    ours, theirs = refs[:far], refs[far : 2 * far - WHOLE]
    own, near, whole, *coded = refs[2 * far - WHOLE :]
    mine = (ours[far - 1].shape[0] - RECORD) // 4
    cap = mine // far // 2 * 2
    half = cap // 2
    rows = 2 * mine
    lane, line = iota((rows, rows), 1), iota((rows, rows), 0)
    mask = line % mine // half * cap + line // mine * half + line % half == lane
    firsts, seconds, projs = [], [], []
    for k in range(far):
        for g in range(2):
            block, at = (ours[k], 4 * mine * g) if k < WHOLE or g == 0 else (theirs[k - WHOLE], 0)
            quarters = [block[at + i * mine : at + (i + 1) * mine] for i in range(4)]
            firsts.append(jnp.concatenate(quarters[:2], axis=1))
            seconds.append(jnp.concatenate(quarters[2:], axis=1))
        at = ours[k].shape[0] - RECORD
        record = ours[k][at : at + RECORD].astype(F32)
        low = jnp.where(mask, record[ROW_LOW : ROW_LOW + 1], 0.0)
        projs.append(jnp.sum(low, axis=1, keepdims=True))
    first, second = jnp.concatenate(firsts, axis=0), jnp.concatenate(seconds, axis=0)
    proj = jnp.concatenate(projs, axis=0).astype(jnp.int32) % E
    total = None
    for e in range(E):
        here = dot_nt(first, own[e]) + dot_nt(second, near[e])
        total = here if total is None else jnp.where(proj == e, here, total)

    def rows_for(j):
        pieces = []
        for y in range(2):
            for n in range(far):
                for g in range(2):
                    start = (j ^ n) * rows + g * mine + n * cap + y * half
                    pieces.append(total[start : start + half])
        return jnp.concatenate(pieces, axis=0)

    whole[...] = rows_for(0)
    diagonal = line == lane
    for j in range(1, far):
        part = rows_for(j)
        top = jnp.max(jnp.abs(part), axis=1, keepdims=True)
        power = jnp.floor(jnp.log(jnp.maximum(top, 2.0**-100)) * (1 / math.log(2))) + 1.0
        level = jnp.abs(part) * jnp.exp2(-power)
        root = level * lax.rsqrt(jnp.maximum(level, 1e-30)) * FULL
        code = jnp.floor(jnp.where(part < 0, -root, root) + 0.5)
        powers = jnp.sum(jnp.where(diagonal, power, 0.0), axis=0, keepdims=True)
        powers = jnp.broadcast_to(powers, (RECORD, rows))
        block = jnp.concatenate([code[:, :128], code[:, 128:], powers], axis=0)
        coded[j - 1][...] = block.astype(jnp.int32).astype(jnp.int16)


def lookup_kernel(far, *refs):
    blocks, (values, near_values), (fetched, records, value_rows) = (
        refs[:far],
        refs[far : far + 2],
        refs[far + 2 :],
    )
    rows = records.shape[0]
    group = rows // far
    lane, line = iota((rows, rows), 1), iota((rows, rows), 0)
    total = jnp.zeros((RECORD, rows), F32)
    for n in range(far):
        at = blocks[n].shape[0] - RECORD
        tile = blocks[n][at : at + RECORD]
        source = n * group + lane // (rows // 2) * (group // 2) + lane % (group // 2)
        inside = lane // (group // 2) % far == n
        move = jnp.where(jnp.logical_and(line == source, inside), 1.0, 0.0).astype(BF16)
        total = total + dot_nn(tile, move)
    value_row = KC * total[ROW_HIGH : ROW_HIGH + 1] + total[ROW_LOW : ROW_LOW + 1]
    value_rows[...] = jnp.broadcast_to(value_row, value_rows.shape)
    padded = jnp.concatenate([total, jnp.zeros((rows - RECORD, rows), F32)], axis=0).astype(BF16)
    column = dot_nt(jnp.where(line == lane, 1.0, 0.0).astype(BF16), padded)
    records[...] = column
    row = KC * column[:, ROW_HIGH : ROW_HIGH + 1] + column[:, ROW_LOW : ROW_LOW + 1]
    hot = iota((rows, values.shape[0]), 1) == row.astype(jnp.int32)
    hot = jnp.where(hot, 1.0, 0.0).astype(BF16)
    fetched[: rows // 2] = dot_nn(hot[: rows // 2], values[...])
    fetched[rows // 2 :] = dot_nn(hot[rows // 2 :], near_values[...])


def reduce_kernel(far, *refs):
    (whole, fetched, records, value_rows), coded, (contrib, pass_on, back) = (
        refs[:4],
        refs[4 : 3 + far],
        refs[3 + far :],
    )
    z, x, c = place()
    rows, width = whole.shape
    half = rows // far // 4
    line, lane = iota((rows, rows), 0), iota((rows, rows), 1)
    diagonal = line == lane
    total = whole[...]
    for block in coded:
        code = block[...].astype(jnp.int32).astype(F32)
        power = jnp.where(diagonal, code[2 * rows : 2 * rows + 1], 0.0)
        scale = jnp.exp2(jnp.sum(power, axis=1, keepdims=True)) * (1 / FULL**2)
        value = jnp.concatenate([code[:rows], code[rows : 2 * rows]], axis=1)
        total = total + value * jnp.abs(value) * scale
    pair_grad = total.astype(BF16).astype(F32)
    record = records[...]
    share = record[:, SCORE : SCORE + 1] * pair_grad
    contrib[...] = share[: rows // 2].astype(BF16)
    send = value_rows[0:1]
    send_high = jnp.floor(send * (1 / KC))
    tile = iota((RECORD, width), 0)
    spare = jnp.zeros((1, width - rows), F32)
    high_row = jnp.concatenate([send_high, spare], axis=1)
    low_row = jnp.concatenate([send - KC * send_high, spare], axis=1)
    tail = jnp.where(tile == 0, high_row, jnp.where(tile == 1, low_row, 0.0))
    pass_on[...] = jnp.concatenate([share[rows // 2 :], tail], axis=0).astype(BF16)
    dscore = jnp.sum(pair_grad * fetched[...], axis=1, keepdims=True)
    owner = z * 2 + (line // (rows // 2) ^ x)
    target = owner * (2 * half) + (line // half % 2 ^ c) * half + line % half
    spread = jnp.where(lane == target, dscore, 0.0).reshape(2, far, 2 * half, rows)
    spread = jnp.sum(spread[0] + spread[1], axis=1)
    outer = jnp.sum(dscore * record, axis=0, keepdims=True)
    empty = jnp.zeros((7 - far, rows), F32)
    block = jnp.concatenate([spread, outer, empty], axis=0)
    for k in range(back.shape[0]):
        back[k] = block


def output_kernel(far, contrib, passed, value_rows, back, scaled, hits, *outs):
    out, row_out, col_out, core_out = outs
    half = contrib.shape[0]
    rows = 2 * half
    tail = passed[half : half + RECORD].astype(F32)
    lane = iota((1, rows), 1)
    other = (KC * tail[0:1] + tail[1:2])[:, :rows]
    row = jnp.where(lane < half, value_rows[0:1], other).astype(jnp.int32)
    hot = jnp.where(iota((out.shape[0], rows), 0) == row, 1.0, 0.0).astype(BF16)
    out[...] = dot_nn(hot, jnp.concatenate([contrib[...], passed[:half]], axis=0))
    z, x, _ = place()
    line = iota(back.shape[1:], 0)
    total = jnp.zeros(back.shape[1:], F32)
    for k in range(back.shape[0]):
        mine = jnp.logical_and(line == (k // 4 ^ z), k // 2 % 2 == x)
        total = total + jnp.where(jnp.logical_or(mine, line == far), back[k], 0.0)
    dscore = jnp.sum(total[:far], axis=0, keepdims=True)
    outer = total[far : far + 1]
    grads = add_thirds(dot_nt(thirds(scaled[...] * dscore), hits[...]))
    split = row_out.shape[0]
    row_out[...] = grads[:split]
    col_out[...] = grads[split:]
    r, s = iota((RANK, RANK), 0), iota((RANK, RANK), 1)
    result = jnp.zeros((RANK, RANK), F32)
    for k in range(RANK * RANK):
        mask = jnp.logical_or(lane == OUTER + k, lane == OUTER_REST + k)
        value = jnp.sum(jnp.where(mask, outer, 0.0), axis=1, keepdims=True)
        result = jnp.where(r * RANK + s == k, value, result)
    core_out[...] = result


VMEM = pl.BlockSpec(memory_space=pltpu.VMEM)
HBM = pl.BlockSpec(memory_space=pltpu.HBM)


def call(kernel, name, outs, ins, flops, moved, scratch=(), limit=24):
    return pl.pallas_call(
        kernel,
        name=name,
        out_shape=outs,
        in_specs=ins,
        out_specs=jax.tree.map(lambda _: VMEM, outs),
        scratch_shapes=scratch,
        cost_estimate=pl.CostEstimate(flops=flops, bytes_accessed=moved, transcendentals=0),
        compiler_params=pltpu.CompilerParams(vmem_limit_bytes=limit << 20),
    )


def shape(dims, kind):
    return jax.ShapeDtypeStruct(dims, kind)


def local_pairs(grads, values, expand_weight, row_factors, col_factors, core, pair_index, counts):
    far = lax.axis_size("far")
    nmem = 2 * far
    tokens, depth = grads.shape
    vrows, width = values.shape
    rows = pair_index.shape[1]
    factors = NR * RANK + NC * RANK
    swap = [(0, 1), (1, 0)]

    def along_far(block, k):
        return lax.ppermute(block, "far", [(i, i ^ k) for i in range(far)])

    near_weight = lax.ppermute(expand_weight, "near", swap)
    blocks = [shape(((4 if k < WHOLE else 2) * rows + RECORD, 128), BF16) for k in range(far)]

    def prepare(name, first, last, extra, limit):
        extras = (shape((factors, rows), F32), shape((tokens, rows), BF16)) if extra else ()
        return call(
            functools.partial(prepare_kernel, far, first, last, extra),
            name,
            tuple(blocks[first:last]) + extras,
            [HBM] * 6,
            rows * tokens * depth,
            2 * tokens * depth,
            (
                pltpu.VMEM((2, rows), jnp.int32),
                pltpu.VMEM((1, nmem), jnp.int32),
                pltpu.VMEM((RANK, RANK), F32),
                pltpu.VMEM((NR * RANK, tokens), F32),
                pltpu.VMEM((NC * RANK, tokens), F32),
                pltpu.VMEM((tokens, depth), BF16),
                pltpu.SemaphoreType.DMA((6,)),
            ),
            limit,
        )(pair_index, counts.reshape(1, nmem), core, row_factors.T, col_factors.T, grads)

    sends = (None,) + tuple(prepare("prepare", 1, far, False, 60))
    own_block, scaled, hits = prepare("prepare_own", 0, 1, True, 24)
    got = {k: along_far(sends[k], k) for k in reversed(range(1, far))}
    ours = [own_block] + [got[k] for k in range(1, far)]
    theirs = [lax.ppermute(block, "col", swap) for block in ours[WHOLE:]]
    near_values = lax.ppermute(values, "near", swap)
    code = shape((2 * rows + RECORD, 128), jnp.int16)
    whole, *coded = call(
        functools.partial(project_kernel, far),
        "project",
        (shape((rows, width), F32),) + (code,) * (far - 1),
        [VMEM] * (2 * far - WHOLE + 2),
        4 * E * far * rows * depth // far * width,
        8 * E * width * depth // nmem,
    )(*ours, *theirs, expand_weight, near_weight)
    coded = [along_far(coded[j - 1], j) for j in reversed(range(1, far))]
    fetched, records, value_rows = call(
        functools.partial(lookup_kernel, far),
        "lookup",
        (shape((rows, width), F32), shape((rows, rows), F32), shape((8, rows), F32)),
        [VMEM] * (far + 2),
        2 * rows * vrows * width,
        4 * vrows * width,
    )(*ours, values, near_values)
    contrib, pass_on, back = call(
        functools.partial(reduce_kernel, far),
        "reduce",
        (
            shape((rows // 2, width), BF16),
            shape((rows // 2 + RECORD, width), BF16),
            shape((2 * nmem, 8, rows), F32),
        ),
        [VMEM] * (3 + far),
        8 * rows * width,
        10 * rows * width,
    )(whole, fetched, records, value_rows, *coded)
    back = lax.all_to_all(back, ("far", "near", "col"), split_axis=0, concat_axis=0, tiled=True)
    passed = lax.ppermute(pass_on, "near", swap)
    value_grad, row_grad, col_grad, core_grad = call(
        functools.partial(output_kernel, far),
        "outputs",
        (
            shape((vrows, width), F32),
            shape((NR * RANK, tokens), F32),
            shape((NC * RANK, tokens), F32),
            shape((RANK, RANK), F32),
        ),
        [VMEM] * 6,
        2 * rows * vrows * width,
        4 * vrows * width,
    )(contrib, passed, value_rows, back, scaled, hits)
    return value_grad, row_grad.T, col_grad.T, core_grad


def solution(mesh):
    ngroup, nmem, ncol = (mesh.shape[a] for a in ("group", "mem", "col"))

    def run(*args):
        rows = args[6].shape[1] // (ngroup * nmem)
        depth = args[0].shape[1]
        fits = nmem % 2 == 0 and ncol == 2 and rows == 16 * nmem == 128
        fits = fits and depth == 256 * nmem and args[1].shape[1] == 256 * ncol
        if fits and nmem * rows <= E * depth:
            used = Mesh(
                mesh.devices.reshape(ngroup, nmem // 2, 2, ncol), ("group", "far", "near", "col")
            )
            mem, body = ("far", "near"), local_pairs
        else:
            used, mem, body = mesh, ("mem",), local_weights
        both = ("group",) + mem
        return jax.shard_map(
            body,
            mesh=used,
            in_specs=(
                P(both, None),
                P(mem, "col"),
                P(None, "col", mem),
                P(both, None),
                P(both, None),
                P(),
                P(None, both),
                P(both),
            ),
            out_specs=(
                P(both, "col"),
                P(both, None),
                P(both, None),
                P("group", None),
            ),
            check_vma=False,
        )(*args)

    return run
```

```python
import functools
import math

import jax
import jax.numpy as jnp
from jax import lax
from jax.experimental import pallas as pl
from jax.experimental.pallas import tpu as pltpu
from jax.sharding import Mesh
from jax.sharding import PartitionSpec as P

E = 4
RANK = 2
NR = 8
NC = 8
KC = 64
F32 = jnp.float32
BF16 = jnp.bfloat16

SCORE, ROW_HIGH, ROW_LOW, OUTER, OUTER_REST = 0, 1, 2, 4, 12
RECORD = 16
FULL = 32000.0
WHOLE = 2


def local_weights(grads, values, expand_weight, row_factors, col_factors, core, pair_index, counts):
    nmem = lax.axis_size("mem")
    tokens = grads.shape[0]
    width = values.shape[1]
    vrows = values.shape[0]
    rows = pair_index.shape[1]
    cap = rows // nmem
    high = lax.Precision.HIGHEST
    expanded = jnp.einsum(
        "tn,evn->tev",
        grads,
        lax.all_gather(expand_weight, "mem", axis=2, tiled=True),
        preferred_element_type=jnp.float32,
    ).astype(jnp.bfloat16)
    code = pair_index[0]
    local_row = pair_index[1]
    within = jnp.tile(jnp.arange(cap, dtype=jnp.int32), nmem)
    owner = jnp.repeat(jnp.arange(nmem, dtype=jnp.int32), cap)
    live = within < counts[owner]
    token = code // (NR * NC)
    row_cand = code // NC % NR
    col_cand = code % NC
    a_p = row_factors.reshape(tokens, NR, RANK)[token, row_cand]
    b_p = col_factors.reshape(tokens, NC, RANK)[token, col_cand]
    core_b = jnp.dot(b_p, core.T, precision=high)
    core_a = jnp.dot(a_p, core, precision=high)
    score = jnp.where(live, jnp.sum(a_p * core_b, -1), 0.0).astype(jnp.bfloat16)
    proj = local_row % KC % E
    pair_grad = jnp.where(live[:, None], expanded[token, proj], jnp.zeros((), jnp.bfloat16))
    got_row = lax.all_to_all(
        local_row.reshape(nmem, cap), "mem", split_axis=0, concat_axis=0, tiled=True
    ).reshape(rows)
    fetched = lax.all_to_all(
        values[got_row].reshape(nmem, cap, width), "mem", split_axis=0, concat_axis=0, tiled=True
    ).reshape(rows, width)
    own_contrib = (score.astype(jnp.float32)[:, None] * pair_grad.astype(jnp.float32)).astype(
        jnp.bfloat16
    )
    contrib = lax.all_to_all(
        own_contrib.reshape(nmem, cap, width), "mem", split_axis=0, concat_axis=0, tiled=True
    ).reshape(rows, width)
    dscore = jnp.einsum("pv,pv->p", pair_grad, fetched, preferred_element_type=jnp.float32)
    block = min(2048, rows)

    def add_block(step, total):
        onehot = (jnp.arange(vrows, dtype=jnp.int32)[:, None] == got_row[None, :]).astype(
            jnp.bfloat16
        )
        return total + jnp.dot(onehot, contrib, preferred_element_type=jnp.float32)

    value_grad = lax.fori_loop(0, rows // block, add_block, jnp.zeros((vrows, width), jnp.float32))
    dscore = lax.psum(dscore, "col")
    row_grad = jax.ops.segment_sum(
        dscore[:, None] * core_b, token * NR + row_cand, num_segments=tokens * NR
    )
    col_grad = jax.ops.segment_sum(
        dscore[:, None] * core_a, token * NC + col_cand, num_segments=tokens * NC
    )
    row_grad = row_grad.reshape(tokens, NR * RANK)
    col_grad = col_grad.reshape(tokens, NC * RANK)
    core_part = jnp.dot((dscore[:, None] * a_p).T, b_p, precision=high)
    core_grad = lax.psum(core_part, "mem")
    return (value_grad, row_grad, col_grad, core_grad)


def iota(shape, dim):
    return lax.broadcasted_iota(jnp.int32, shape, dim)


def dot_nn(x, y):
    return jnp.dot(x, y, preferred_element_type=F32)


def dot_nt(x, y):
    return lax.dot_general(x, y, (((1,), (1,)), ((), ())), preferred_element_type=F32)


def thirds(x):
    first = x.astype(BF16)
    rest = x - first.astype(F32)
    second = rest.astype(BF16)
    third = (rest - second.astype(F32)).astype(BF16)
    return jnp.concatenate([first, second, third], axis=0)


def add_thirds(y):
    n = y.shape[0] // 3
    return (y[2 * n :] + y[n : 2 * n]) + y[:n]


def place():
    return lax.axis_index("far"), lax.axis_index("near"), lax.axis_index("col")


def prepare_kernel(far, first, last, extra, *refs):
    sources, refs = refs[:6], refs[6:]
    sends, refs = refs[: last - first], refs[last - first :]
    if extra:
        (scaled, hits), refs = refs[:2], refs[2:]
    targets, sems = refs[:6], refs[6]
    pair, counts, core, row_fac, col_fac, grads = targets
    copies = [
        pltpu.make_async_copy(source, target, sems.at[k])
        for k, (source, target) in enumerate(zip(sources, targets))
    ]
    for copy in copies:
        copy.start()
    for copy in copies[:-1]:
        copy.wait()
    z, x, c = place()
    nmem = 2 * far
    rows = pair.shape[1]
    cap = rows // nmem
    half = cap // 2
    tokens, depth = grads.shape
    shard = depth // nmem
    code = pair[0:1, :]
    local_row = pair[1:2, :]
    lane = iota((1, rows), 1)
    owner = lane // cap
    limit = jnp.zeros((1, rows), jnp.int32)
    for o in range(nmem):
        limit = jnp.where(owner == o, counts[0:1, o : o + 1], limit)
    live = lane % cap < limit
    token = code // (NR * NC)
    row_cand = code // NC % NR
    col_cand = code % NC
    hit = iota((tokens, rows), 0) == token
    hot = jnp.where(hit, 1.0, 0.0).astype(BF16)
    factors = jnp.concatenate([row_fac[...], col_fac[...]], axis=0)
    found = add_thirds(dot_nn(thirds(factors), hot))
    at = iota(found.shape, 0)
    split = NR * RANK

    def pick(row):
        return jnp.sum(jnp.where(at == row, found, 0.0), axis=0, keepdims=True)

    a0, a1 = pick(row_cand * RANK), pick(row_cand * RANK + 1)
    b0, b1 = pick(split + col_cand * RANK), pick(split + col_cand * RANK + 1)
    c00, c01, c10, c11 = core[0:1, 0:1], core[0:1, 1:2], core[1:2, 0:1], core[1:2, 1:2]
    core_b0, core_b1 = c00 * b0 + c01 * b1, c10 * b0 + c11 * b1
    score = jnp.where(live, a0 * core_b0 + a1 * core_b1, 0.0)
    if extra:
        hits[...] = hot
        core_a0, core_a1 = c00 * a0 + c10 * a1, c01 * a0 + c11 * a1
        even = at % RANK == 0
        of_row = jnp.where(at // RANK == row_cand, jnp.where(even, core_b0, core_b1), 0.0)
        of_col = jnp.where((at - split) // RANK == col_cand, jnp.where(even, core_a0, core_a1), 0.0)
        scaled[...] = jnp.where(at < split, of_row, of_col)

    field = iota((RECORD, rows), 0)
    record = jnp.where(field == SCORE, score, 0.0)
    record = jnp.where(field == ROW_HIGH, (local_row // KC).astype(F32), record)
    record = jnp.where(field == ROW_LOW, (local_row % KC).astype(F32), record)
    for k, outer in enumerate((a0 * b0, a0 * b1, a1 * b0, a1 * b1)):
        top = outer.astype(BF16).astype(F32)
        record = jnp.where(field == OUTER + k, top, record)
        record = jnp.where(field == OUTER_REST + k, outer - top, record)

    to = iota((rows, rows), 1)
    to_m, to_y = to // (2 * cap), to // cap % 2
    to_pair = ((to_m ^ z) * 2 + (to_y ^ x)) * cap + (to // half % 2 ^ c) * half + to % half
    order = jnp.where(iota((rows, rows), 0) == to_pair, 1.0, 0.0).astype(BF16)
    records = dot_nn(record.astype(BF16), order).astype(BF16)

    q = iota((rows, rows), 0)
    mine = rows // 2
    q_pair = ((q % mine // cap ^ z) * 2 + (q // half % 2 ^ x)) * cap
    q_pair = q_pair + (q // mine ^ c) * half + q % half
    take = jnp.where(iota((rows, rows), 1) == q_pair, 1.0, 0.0).astype(BF16)
    live_hits = jnp.where(jnp.logical_and(hit, live), 1.0, 0.0).astype(BF16)
    chosen = dot_nt(take, live_hits).astype(BF16)
    copies[-1].wait()
    for k in range(first, last):
        taken = []
        for y in range(2):
            start = pl.multiple_of(((z ^ k) * 2 + (x ^ y)) * shard, shard)
            part = grads[:, pl.ds(start, shard)]
            taken.append(dot_nn(chosen if k < WHOLE else chosen[:mine], part).astype(BF16))
        blocks = []
        for g in range(2 if k < WHOLE else 1):
            for part in taken:
                part = part[g * mine : (g + 1) * mine]
                blocks += [part[:, :128], part[:, 128:]]
        sends[k - first][...] = jnp.concatenate(blocks + [records], axis=0)


def project_kernel(far, *refs):
    ours, theirs = refs[:far], refs[far : 2 * far - WHOLE]
    own, near, whole, *coded = refs[2 * far - WHOLE :]
    mine = (ours[far - 1].shape[0] - RECORD) // 4
    cap = mine // far // 2 * 2
    half = cap // 2
    rows = 2 * mine
    lane, line = iota((rows, rows), 1), iota((rows, rows), 0)
    mask = line % mine // half * cap + line // mine * half + line % half == lane
    firsts, seconds, projs = [], [], []
    for k in range(far):
        for g in range(2):
            block, at = (ours[k], 4 * mine * g) if k < WHOLE or g == 0 else (theirs[k - WHOLE], 0)
            quarters = [block[at + i * mine : at + (i + 1) * mine] for i in range(4)]
            firsts.append(jnp.concatenate(quarters[:2], axis=1))
            seconds.append(jnp.concatenate(quarters[2:], axis=1))
        at = ours[k].shape[0] - RECORD
        record = ours[k][at : at + RECORD].astype(F32)
        low = jnp.where(mask, record[ROW_LOW : ROW_LOW + 1], 0.0)
        projs.append(jnp.sum(low, axis=1, keepdims=True))
    first, second = jnp.concatenate(firsts, axis=0), jnp.concatenate(seconds, axis=0)
    proj = jnp.concatenate(projs, axis=0).astype(jnp.int32) % E
    total = None
    for e in range(E):
        here = dot_nt(first, own[e]) + dot_nt(second, near[e])
        total = here if total is None else jnp.where(proj == e, here, total)

    def rows_for(j):
        pieces = []
        for y in range(2):
            for n in range(far):
                for g in range(2):
                    start = (j ^ n) * rows + g * mine + n * cap + y * half
                    pieces.append(total[start : start + half])
        return jnp.concatenate(pieces, axis=0)

    whole[...] = rows_for(0)
    diagonal = line == lane
    for j in range(1, far):
        part = rows_for(j)
        top = jnp.max(jnp.abs(part), axis=1, keepdims=True)
        power = jnp.floor(jnp.log(jnp.maximum(top, 2.0**-100)) * (1 / math.log(2))) + 1.0
        level = jnp.abs(part) * jnp.exp2(-power)
        root = level * lax.rsqrt(jnp.maximum(level, 1e-30)) * FULL
        code = jnp.floor(jnp.where(part < 0, -root, root) + 0.5)
        powers = jnp.sum(jnp.where(diagonal, power, 0.0), axis=0, keepdims=True)
        powers = jnp.broadcast_to(powers, (RECORD, rows))
        block = jnp.concatenate([code[:, :128], code[:, 128:], powers], axis=0)
        coded[j - 1][...] = block.astype(jnp.int32).astype(jnp.int16)


def lookup_kernel(far, *refs):
    blocks, (values, near_values), (fetched, records, value_rows) = (
        refs[:far],
        refs[far : far + 2],
        refs[far + 2 :],
    )
    rows = records.shape[0]
    group = rows // far
    lane, line = iota((rows, rows), 1), iota((rows, rows), 0)
    total = jnp.zeros((RECORD, rows), F32)
    for n in range(far):
        at = blocks[n].shape[0] - RECORD
        tile = blocks[n][at : at + RECORD]
        source = n * group + lane // (rows // 2) * (group // 2) + lane % (group // 2)
        inside = lane // (group // 2) % far == n
        move = jnp.where(jnp.logical_and(line == source, inside), 1.0, 0.0).astype(BF16)
        total = total + dot_nn(tile, move)
    value_row = KC * total[ROW_HIGH : ROW_HIGH + 1] + total[ROW_LOW : ROW_LOW + 1]
    value_rows[...] = jnp.broadcast_to(value_row, value_rows.shape)
    padded = jnp.concatenate([total, jnp.zeros((rows - RECORD, rows), F32)], axis=0).astype(BF16)
    column = dot_nt(jnp.where(line == lane, 1.0, 0.0).astype(BF16), padded)
    records[...] = column
    row = KC * column[:, ROW_HIGH : ROW_HIGH + 1] + column[:, ROW_LOW : ROW_LOW + 1]
    hot = iota((rows, values.shape[0]), 1) == row.astype(jnp.int32)
    hot = jnp.where(hot, 1.0, 0.0).astype(BF16)
    fetched[: rows // 2] = dot_nn(hot[: rows // 2], values[...])
    fetched[rows // 2 :] = dot_nn(hot[rows // 2 :], near_values[...])


def reduce_kernel(far, *refs):
    (whole, fetched, records, value_rows), coded, (contrib, pass_on, back) = (
        refs[:4],
        refs[4 : 3 + far],
        refs[3 + far :],
    )
    z, x, c = place()
    rows, width = whole.shape
    half = rows // far // 4
    line, lane = iota((rows, rows), 0), iota((rows, rows), 1)
    diagonal = line == lane
    total = whole[...]
    for block in coded:
        code = block[...].astype(jnp.int32).astype(F32)
        power = jnp.where(diagonal, code[2 * rows : 2 * rows + 1], 0.0)
        scale = jnp.exp2(jnp.sum(power, axis=1, keepdims=True)) * (1 / FULL**2)
        value = jnp.concatenate([code[:rows], code[rows : 2 * rows]], axis=1)
        total = total + value * jnp.abs(value) * scale
    pair_grad = total.astype(BF16).astype(F32)
    record = records[...]
    share = record[:, SCORE : SCORE + 1] * pair_grad
    contrib[...] = share[: rows // 2].astype(BF16)
    send = value_rows[0:1]
    send_high = jnp.floor(send * (1 / KC))
    tile = iota((RECORD, width), 0)
    spare = jnp.zeros((1, width - rows), F32)
    high_row = jnp.concatenate([send_high, spare], axis=1)
    low_row = jnp.concatenate([send - KC * send_high, spare], axis=1)
    tail = jnp.where(tile == 0, high_row, jnp.where(tile == 1, low_row, 0.0))
    pass_on[...] = jnp.concatenate([share[rows // 2 :], tail], axis=0).astype(BF16)
    dscore = jnp.sum(pair_grad * fetched[...], axis=1, keepdims=True)
    owner = z * 2 + (line // (rows // 2) ^ x)
    target = owner * (2 * half) + (line // half % 2 ^ c) * half + line % half
    spread = jnp.where(lane == target, dscore, 0.0).reshape(2, far, 2 * half, rows)
    spread = jnp.sum(spread[0] + spread[1], axis=1)
    outer = jnp.sum(dscore * record, axis=0, keepdims=True)
    empty = jnp.zeros((7 - far, rows), F32)
    block = jnp.concatenate([spread, outer, empty], axis=0)
    for k in range(back.shape[0]):
        back[k] = block


def output_kernel(far, order, contrib, passed, value_rows, back, scaled, hits, *outs):
    out, row_out, col_out, core_out = outs
    half = contrib.shape[0]
    rows = 2 * half
    tail = passed[half : half + RECORD].astype(F32)
    lane = iota((1, rows), 1)
    other = (KC * tail[0:1] + tail[1:2])[:, :rows]
    row = jnp.where(lane < half, value_rows[0:1], other).astype(jnp.int32)
    hot = jnp.where(iota((out.shape[0], rows), 0) == row, 1.0, 0.0).astype(BF16)
    out[...] = dot_nn(hot, jnp.concatenate([contrib[...], passed[:half]], axis=0))
    z, x, _ = place()
    line = iota(back.shape[1:], 0)
    total = jnp.zeros(back.shape[1:], F32)
    for k in range(back.shape[0]):
        sender = order[k]
        mine = jnp.logical_and(line == (sender // 4 ^ z), sender // 2 % 2 == x)
        total = total + jnp.where(jnp.logical_or(mine, line == far), back[k], 0.0)
    dscore = jnp.sum(total[:far], axis=0, keepdims=True)
    outer = total[far : far + 1]
    grads = add_thirds(dot_nt(thirds(scaled[...] * dscore), hits[...]))
    split = row_out.shape[0]
    row_out[...] = grads[:split]
    col_out[...] = grads[split:]
    r, s = iota((RANK, RANK), 0), iota((RANK, RANK), 1)
    result = jnp.zeros((RANK, RANK), F32)
    for k in range(RANK * RANK):
        mask = jnp.logical_or(lane == OUTER + k, lane == OUTER_REST + k)
        value = jnp.sum(jnp.where(mask, outer, 0.0), axis=1, keepdims=True)
        result = jnp.where(r * RANK + s == k, value, result)
    core_out[...] = result


VMEM = pl.BlockSpec(memory_space=pltpu.VMEM)
HBM = pl.BlockSpec(memory_space=pltpu.HBM)


def call(kernel, name, outs, ins, flops, moved, scratch=(), limit=24):
    return pl.pallas_call(
        kernel,
        name=name,
        out_shape=outs,
        in_specs=ins,
        out_specs=jax.tree.map(lambda _: VMEM, outs),
        scratch_shapes=scratch,
        cost_estimate=pl.CostEstimate(flops=flops, bytes_accessed=moved, transcendentals=0),
        compiler_params=pltpu.CompilerParams(vmem_limit_bytes=limit << 20),
    )


def shape(dims, kind):
    return jax.ShapeDtypeStruct(dims, kind)


def local_pairs(grads, values, expand_weight, row_factors, col_factors, core, pair_index, counts):
    far = lax.axis_size("far")
    nmem = 2 * far
    tokens, depth = grads.shape
    vrows, width = values.shape
    rows = pair_index.shape[1]
    factors = NR * RANK + NC * RANK
    swap = [(0, 1), (1, 0)]

    def along_far(block, k):
        return lax.ppermute(block, "far", [(i, i ^ k) for i in range(far)])

    near_weight = lax.ppermute(expand_weight, "near", swap)
    blocks = [shape(((4 if k < WHOLE else 2) * rows + RECORD, 128), BF16) for k in range(far)]

    operands = (pair_index, counts.reshape(1, nmem), core, row_factors.T, col_factors.T, grads)

    def prepare(name, first, last, extra, limit):
        extras = (shape((factors, rows), F32), shape((tokens, rows), BF16)) if extra else ()
        return call(
            functools.partial(prepare_kernel, far, first, last, extra),
            name,
            tuple(blocks[first:last]) + extras,
            [HBM] * 6,
            rows * tokens * depth,
            2 * tokens * depth,
            (
                pltpu.VMEM((2, rows), jnp.int32),
                pltpu.VMEM((1, nmem), jnp.int32),
                pltpu.VMEM((RANK, RANK), F32),
                pltpu.VMEM((NR * RANK, tokens), F32),
                pltpu.VMEM((NC * RANK, tokens), F32),
                pltpu.VMEM((tokens, depth), BF16),
                pltpu.SemaphoreType.DMA((6,)),
            ),
            limit,
        )(*(pltpu.with_memory_space_constraint(a, pltpu.HBM) for a in operands))

    own_block, *sends, scaled, hits = prepare("prepare", 0, far, True, 24)
    sends = [None] + sends
    got = {k: along_far(sends[k], k) for k in reversed(range(1, far))}
    ours = [own_block] + [got[k] for k in range(1, far)]
    theirs = [lax.ppermute(block, "col", swap) for block in ours[WHOLE:]]
    near_values = lax.ppermute(values, "near", swap)
    code = shape((2 * rows + RECORD, 128), jnp.int16)
    whole, *coded = call(
        functools.partial(project_kernel, far),
        "project",
        (shape((rows, width), F32),) + (code,) * (far - 1),
        [VMEM] * (2 * far - WHOLE + 2),
        4 * E * far * rows * depth // far * width,
        8 * E * width * depth // nmem,
    )(*ours, *theirs, expand_weight, near_weight)
    coded = [along_far(coded[j - 1], j) for j in reversed(range(1, far))]
    fetched, records, value_rows = call(
        functools.partial(lookup_kernel, far),
        "lookup",
        (shape((rows, width), F32), shape((rows, rows), F32), shape((8, rows), F32)),
        [VMEM] * (far + 2),
        2 * rows * vrows * width,
        4 * vrows * width,
    )(*ours, values, near_values)
    contrib, pass_on, back = call(
        functools.partial(reduce_kernel, far),
        "reduce",
        (
            shape((rows // 2, width), BF16),
            shape((rows // 2 + RECORD, width), BF16),
            shape((2 * nmem, 8, rows), F32),
        ),
        [VMEM] * (3 + far),
        8 * rows * width,
        10 * rows * width,
    )(whole, fetched, records, value_rows, *coded)
    fars = [*range(far // 2 - 1, far), *range(far // 2 - 1)]
    order = [4 * z + k for z in fars for k in (3, 2, 1, 0)]
    back = lax.all_to_all(
        back,
        ("far", "near", "col"),
        split_axis=0,
        concat_axis=0,
        axis_index_groups=[order],
        tiled=True,
    )
    passed = lax.ppermute(pass_on, "near", swap)
    value_grad, row_grad, col_grad, core_grad = call(
        functools.partial(output_kernel, far, order),
        "outputs",
        (
            shape((vrows, width), F32),
            shape((NR * RANK, tokens), F32),
            shape((NC * RANK, tokens), F32),
            shape((RANK, RANK), F32),
        ),
        [VMEM] * 6,
        2 * rows * vrows * width,
        4 * vrows * width,
    )(contrib, passed, value_rows, back, scaled, hits)
    return value_grad, row_grad.T, col_grad.T, core_grad


def solution(mesh):
    ngroup, nmem, ncol = (mesh.shape[a] for a in ("group", "mem", "col"))

    def run(*args):
        rows = args[6].shape[1] // (ngroup * nmem)
        depth = args[0].shape[1]
        fits = nmem % 2 == 0 and ncol == 2 and rows == 16 * nmem == 128
        fits = fits and depth == 256 * nmem and args[1].shape[1] == 256 * ncol
        if fits and nmem * rows <= E * depth:
            used = Mesh(
                mesh.devices.reshape(ngroup, nmem // 2, 2, ncol), ("group", "far", "near", "col")
            )
            mem, body = ("far", "near"), local_pairs
        else:
            used, mem, body = mesh, ("mem",), local_weights
        both = ("group",) + mem
        return jax.shard_map(
            body,
            mesh=used,
            in_specs=(
                P(both, None),
                P(mem, "col"),
                P(None, "col", mem),
                P(both, None),
                P(both, None),
                P(),
                P(None, both),
                P(both),
            ),
            out_specs=(
                P(both, "col"),
                P(both, None),
                P(both, None),
                P("group", None),
            ),
            check_vma=False,
        )(*args)

    return run
```

```python
import functools
import math

import jax
import jax.numpy as jnp
from jax import lax
from jax.experimental import pallas as pl
from jax.experimental.pallas import tpu as pltpu
from jax.sharding import Mesh
from jax.sharding import PartitionSpec as P

E = 4
RANK = 2
NR = 8
NC = 8
KC = 64
F32 = jnp.float32
BF16 = jnp.bfloat16

SCORE, ROW_HIGH, ROW_LOW, OUTER, OUTER_REST = 0, 1, 2, 4, 12
RECORD = 16
FULL = 32000.0
WHOLE = 2


def local_weights(grads, values, expand_weight, row_factors, col_factors, core, pair_index, counts):
    nmem = lax.axis_size("mem")
    tokens = grads.shape[0]
    width = values.shape[1]
    vrows = values.shape[0]
    rows = pair_index.shape[1]
    cap = rows // nmem
    high = lax.Precision.HIGHEST
    expanded = jnp.einsum(
        "tn,evn->tev",
        grads,
        lax.all_gather(expand_weight, "mem", axis=2, tiled=True),
        preferred_element_type=jnp.float32,
    ).astype(jnp.bfloat16)
    code = pair_index[0]
    local_row = pair_index[1]
    within = jnp.tile(jnp.arange(cap, dtype=jnp.int32), nmem)
    owner = jnp.repeat(jnp.arange(nmem, dtype=jnp.int32), cap)
    live = within < counts[owner]
    token = code // (NR * NC)
    row_cand = code // NC % NR
    col_cand = code % NC
    a_p = row_factors.reshape(tokens, NR, RANK)[token, row_cand]
    b_p = col_factors.reshape(tokens, NC, RANK)[token, col_cand]
    core_b = jnp.dot(b_p, core.T, precision=high)
    core_a = jnp.dot(a_p, core, precision=high)
    score = jnp.where(live, jnp.sum(a_p * core_b, -1), 0.0).astype(jnp.bfloat16)
    proj = local_row % KC % E
    pair_grad = jnp.where(live[:, None], expanded[token, proj], jnp.zeros((), jnp.bfloat16))
    got_row = lax.all_to_all(
        local_row.reshape(nmem, cap), "mem", split_axis=0, concat_axis=0, tiled=True
    ).reshape(rows)
    fetched = lax.all_to_all(
        values[got_row].reshape(nmem, cap, width), "mem", split_axis=0, concat_axis=0, tiled=True
    ).reshape(rows, width)
    own_contrib = (score.astype(jnp.float32)[:, None] * pair_grad.astype(jnp.float32)).astype(
        jnp.bfloat16
    )
    contrib = lax.all_to_all(
        own_contrib.reshape(nmem, cap, width), "mem", split_axis=0, concat_axis=0, tiled=True
    ).reshape(rows, width)
    dscore = jnp.einsum("pv,pv->p", pair_grad, fetched, preferred_element_type=jnp.float32)
    block = min(2048, rows)

    def add_block(step, total):
        onehot = (jnp.arange(vrows, dtype=jnp.int32)[:, None] == got_row[None, :]).astype(
            jnp.bfloat16
        )
        return total + jnp.dot(onehot, contrib, preferred_element_type=jnp.float32)

    value_grad = lax.fori_loop(0, rows // block, add_block, jnp.zeros((vrows, width), jnp.float32))
    dscore = lax.psum(dscore, "col")
    row_grad = jax.ops.segment_sum(
        dscore[:, None] * core_b, token * NR + row_cand, num_segments=tokens * NR
    )
    col_grad = jax.ops.segment_sum(
        dscore[:, None] * core_a, token * NC + col_cand, num_segments=tokens * NC
    )
    row_grad = row_grad.reshape(tokens, NR * RANK)
    col_grad = col_grad.reshape(tokens, NC * RANK)
    core_part = jnp.dot((dscore[:, None] * a_p).T, b_p, precision=high)
    core_grad = lax.psum(core_part, "mem")
    return (value_grad, row_grad, col_grad, core_grad)


def iota(shape, dim):
    return lax.broadcasted_iota(jnp.int32, shape, dim)


def dot_nn(x, y):
    return jnp.dot(x, y, preferred_element_type=F32)


def dot_nt(x, y):
    return lax.dot_general(x, y, (((1,), (1,)), ((), ())), preferred_element_type=F32)


def thirds(x):
    first = x.astype(BF16)
    rest = x - first.astype(F32)
    second = rest.astype(BF16)
    third = (rest - second.astype(F32)).astype(BF16)
    return jnp.concatenate([first, second, third], axis=0)


def add_thirds(y):
    n = y.shape[0] // 3
    return (y[2 * n :] + y[n : 2 * n]) + y[:n]


def place():
    return lax.axis_index("far"), lax.axis_index("near"), lax.axis_index("col")


def prepare_kernel(far, *refs):
    sources, sends, (scaled, hits, *targets, sems) = refs[:6], refs[6 : 6 + far], refs[6 + far :]
    pair, counts, core, row_fac, col_fac, grads = targets
    copies = [
        pltpu.make_async_copy(source, target, sems.at[k])
        for k, (source, target) in enumerate(zip(sources, targets))
    ]
    for copy in copies:
        copy.start()
    for copy in copies[:-1]:
        copy.wait()
    z, x, c = place()
    nmem = 2 * far
    rows = pair.shape[1]
    cap = rows // nmem
    half = cap // 2
    tokens, depth = grads.shape
    shard = depth // nmem
    code = pair[0:1, :]
    local_row = pair[1:2, :]
    lane = iota((1, rows), 1)
    owner = lane // cap
    limit = jnp.zeros((1, rows), jnp.int32)
    for o in range(nmem):
        limit = jnp.where(owner == o, counts[0:1, o : o + 1], limit)
    live = lane % cap < limit
    token = code // (NR * NC)
    row_cand = code // NC % NR
    col_cand = code % NC
    hit = iota((tokens, rows), 0) == token
    hot = jnp.where(hit, 1.0, 0.0).astype(BF16)
    factors = jnp.concatenate([row_fac[...], col_fac[...]], axis=0)
    found = add_thirds(dot_nn(thirds(factors), hot))
    at = iota(found.shape, 0)
    split = NR * RANK

    def pick(row):
        return jnp.sum(jnp.where(at == row, found, 0.0), axis=0, keepdims=True)

    a0, a1 = pick(row_cand * RANK), pick(row_cand * RANK + 1)
    b0, b1 = pick(split + col_cand * RANK), pick(split + col_cand * RANK + 1)
    c00, c01, c10, c11 = core[0:1, 0:1], core[0:1, 1:2], core[1:2, 0:1], core[1:2, 1:2]
    core_b0, core_b1 = c00 * b0 + c01 * b1, c10 * b0 + c11 * b1
    score = jnp.where(live, a0 * core_b0 + a1 * core_b1, 0.0)
    hits[...] = hot
    core_a0, core_a1 = c00 * a0 + c10 * a1, c01 * a0 + c11 * a1
    even = at % RANK == 0
    of_row = jnp.where(at // RANK == row_cand, jnp.where(even, core_b0, core_b1), 0.0)
    of_col = jnp.where((at - split) // RANK == col_cand, jnp.where(even, core_a0, core_a1), 0.0)
    scaled[...] = jnp.where(at < split, of_row, of_col)

    field = iota((RECORD, rows), 0)
    record = jnp.where(field == SCORE, score, 0.0)
    record = jnp.where(field == ROW_HIGH, (local_row // KC).astype(F32), record)
    record = jnp.where(field == ROW_LOW, (local_row % KC).astype(F32), record)
    for k, outer in enumerate((a0 * b0, a0 * b1, a1 * b0, a1 * b1)):
        top = outer.astype(BF16).astype(F32)
        record = jnp.where(field == OUTER + k, top, record)
        record = jnp.where(field == OUTER_REST + k, outer - top, record)

    to = iota((rows, rows), 1)
    to_m, to_y = to // (2 * cap), to // cap % 2
    to_pair = ((to_m ^ z) * 2 + (to_y ^ x)) * cap + (to // half % 2 ^ c) * half + to % half
    order = jnp.where(iota((rows, rows), 0) == to_pair, 1.0, 0.0).astype(BF16)
    records = dot_nn(record.astype(BF16), order).astype(BF16)

    q = iota((rows, rows), 0)
    mine = rows // 2
    q_pair = ((q % mine // cap ^ z) * 2 + (q // half % 2 ^ x)) * cap
    q_pair = q_pair + (q // mine ^ c) * half + q % half
    take = jnp.where(iota((rows, rows), 1) == q_pair, 1.0, 0.0).astype(BF16)
    live_hits = jnp.where(jnp.logical_and(hit, live), 1.0, 0.0).astype(BF16)
    chosen = dot_nt(take, live_hits).astype(BF16)
    copies[-1].wait()
    for k in range(far):
        taken = []
        for y in range(2):
            start = pl.multiple_of(((z ^ k) * 2 + (x ^ y)) * shard, shard)
            part = grads[:, pl.ds(start, shard)]
            taken.append(dot_nn(chosen if k < WHOLE else chosen[:mine], part).astype(BF16))
        blocks = []
        for g in range(2 if k < WHOLE else 1):
            for part in taken:
                part = part[g * mine : (g + 1) * mine]
                blocks += [part[:, :128], part[:, 128:]]
        sends[k][...] = jnp.concatenate(blocks + [records], axis=0)


def project_kernel(far, *refs):
    ours, theirs = refs[:far], refs[far : 2 * far - WHOLE]
    own, near, whole, *coded = refs[2 * far - WHOLE :]
    mine = (ours[far - 1].shape[0] - RECORD) // 4
    cap = mine // far // 2 * 2
    half = cap // 2
    rows = 2 * mine
    lane, line = iota((rows, rows), 1), iota((rows, rows), 0)
    mask = line % mine // half * cap + line // mine * half + line % half == lane
    firsts, seconds, projs = [], [], []
    for k in range(far):
        for g in range(2):
            block, at = (ours[k], 4 * mine * g) if k < WHOLE or g == 0 else (theirs[k - WHOLE], 0)
            quarters = [block[at + i * mine : at + (i + 1) * mine] for i in range(4)]
            firsts.append(jnp.concatenate(quarters[:2], axis=1))
            seconds.append(jnp.concatenate(quarters[2:], axis=1))
        at = ours[k].shape[0] - RECORD
        record = ours[k][at : at + RECORD].astype(F32)
        low = jnp.where(mask, record[ROW_LOW : ROW_LOW + 1], 0.0)
        projs.append(jnp.sum(low, axis=1, keepdims=True))
    first, second = jnp.concatenate(firsts, axis=0), jnp.concatenate(seconds, axis=0)
    proj = jnp.concatenate(projs, axis=0).astype(jnp.int32) % E
    total = None
    for e in range(E):
        here = dot_nt(first, own[e]) + dot_nt(second, near[e])
        total = here if total is None else jnp.where(proj == e, here, total)

    def rows_for(j):
        pieces = []
        for y in range(2):
            for n in range(far):
                for g in range(2):
                    start = (j ^ n) * rows + g * mine + n * cap + y * half
                    pieces.append(total[start : start + half])
        return jnp.concatenate(pieces, axis=0)

    whole[...] = rows_for(0)
    diagonal = line == lane
    for j in range(1, far):
        part = rows_for(j)
        top = jnp.max(jnp.abs(part), axis=1, keepdims=True)
        power = jnp.floor(jnp.log(jnp.maximum(top, 2.0**-126)) * (1 / math.log(2))) + 1.0
        level = jnp.abs(part) * jnp.exp2(-power)
        root = level * lax.rsqrt(jnp.maximum(level, 1e-30)) * FULL
        code = jnp.floor(jnp.where(part < 0, -root, root) + 0.5)
        powers = jnp.sum(jnp.where(diagonal, power, 0.0), axis=0, keepdims=True)
        powers = jnp.broadcast_to(powers, (RECORD, rows))
        block = jnp.concatenate([code[:, :128], code[:, 128:], powers], axis=0)
        coded[j - 1][...] = block.astype(jnp.int32).astype(jnp.int16)


def lookup_kernel(far, *refs):
    blocks, (values, near_values), (fetched, records, value_rows) = (
        refs[:far],
        refs[far : far + 2],
        refs[far + 2 :],
    )
    rows = records.shape[0]
    group = rows // far
    lane, line = iota((rows, rows), 1), iota((rows, rows), 0)
    total = jnp.zeros((RECORD, rows), F32)
    for n in range(far):
        at = blocks[n].shape[0] - RECORD
        tile = blocks[n][at : at + RECORD]
        source = n * group + lane // (rows // 2) * (group // 2) + lane % (group // 2)
        inside = lane // (group // 2) % far == n
        move = jnp.where(jnp.logical_and(line == source, inside), 1.0, 0.0).astype(BF16)
        total = total + dot_nn(tile, move)
    value_row = KC * total[ROW_HIGH : ROW_HIGH + 1] + total[ROW_LOW : ROW_LOW + 1]
    value_rows[...] = jnp.broadcast_to(value_row, value_rows.shape)
    padded = jnp.concatenate([total, jnp.zeros((rows - RECORD, rows), F32)], axis=0).astype(BF16)
    column = dot_nt(jnp.where(line == lane, 1.0, 0.0).astype(BF16), padded)
    records[...] = column
    row = KC * column[:, ROW_HIGH : ROW_HIGH + 1] + column[:, ROW_LOW : ROW_LOW + 1]
    hot = iota((rows, values.shape[0]), 1) == row.astype(jnp.int32)
    hot = jnp.where(hot, 1.0, 0.0).astype(BF16)
    fetched[: rows // 2] = dot_nn(hot[: rows // 2], values[...])
    fetched[rows // 2 :] = dot_nn(hot[rows // 2 :], near_values[...])


def reduce_kernel(far, fars, *refs):
    (whole, fetched, records, value_rows), coded, (contrib, pass_on, back) = (
        refs[:4],
        refs[4 : 3 + far],
        refs[3 + far :],
    )
    z, x, c = place()
    rows, width = whole.shape
    half = rows // far // 4
    line, lane = iota((rows, rows), 0), iota((rows, rows), 1)
    diagonal = line == lane
    total = whole[...]
    for block in coded:
        code = block[...].astype(jnp.int32).astype(F32)
        power = jnp.where(diagonal, code[2 * rows : 2 * rows + 1], 0.0)
        scale = jnp.exp2(jnp.sum(power, axis=1, keepdims=True))
        value = jnp.concatenate([code[:rows], code[rows : 2 * rows]], axis=1) * (1 / FULL)
        total = total + value * jnp.abs(value) * scale
    pair_grad = total.astype(BF16).astype(F32)
    record = records[...]
    share = record[:, SCORE : SCORE + 1] * pair_grad
    contrib[...] = share[: rows // 2].astype(BF16)
    send = value_rows[0:1]
    send_high = jnp.floor(send * (1 / KC))
    tile = iota((RECORD, width), 0)
    spare = jnp.zeros((1, width - rows), F32)
    high_row = jnp.concatenate([send_high, spare], axis=1)
    low_row = jnp.concatenate([send - KC * send_high, spare], axis=1)
    tail = jnp.where(tile == 0, high_row, jnp.where(tile == 1, low_row, 0.0))
    pass_on[...] = jnp.concatenate([share[rows // 2 :], tail], axis=0).astype(BF16)
    dscore = jnp.sum(pair_grad * fetched[...], axis=1, keepdims=True)
    owner = z * 2 + (line // (rows // 2) ^ x)
    target = owner * (2 * half) + (line // half % 2 ^ c) * half + line % half
    spread = jnp.where(lane == target, dscore, 0.0).reshape(2, far, 2 * half, rows)
    spread = jnp.sum(spread[0] + spread[1], axis=1)
    outer = jnp.sum(dscore * record, axis=0, keepdims=True)
    low = z < far // 2
    core_row = jnp.where(low, pltpu.roll(outer, rows // 2, 1), outer)
    core_lane = iota((1, rows), 1) - jnp.where(low, rows // 2, 0)
    core_row = jnp.where(jnp.logical_and(core_lane >= 0, core_lane < RECORD), core_row, 0.0)
    for n in range(far):
        for k in range(4):
            row = jnp.where(x == k // 2, spread[n : n + 1], 0.0) + core_row
            rank = sum(jnp.where(z ^ n == far_at, at, 0) for at, far_at in enumerate(fars))
            back[rank * 4 + 3 - k] = row


def output_kernel(far, order, contrib, passed, value_rows, back, scaled, hits, *outs):
    out, row_out, col_out, core_out = outs
    half = contrib.shape[0]
    rows = 2 * half
    tail = passed[half : half + RECORD].astype(F32)
    lane = iota((1, rows), 1)
    other = (KC * tail[0:1] + tail[1:2])[:, :rows]
    row = jnp.where(lane < half, value_rows[0:1], other).astype(jnp.int32)
    hot = jnp.where(iota((out.shape[0], rows), 0) == row, 1.0, 0.0).astype(BF16)
    out[...] = dot_nn(hot, jnp.concatenate([contrib[...], passed[:half]], axis=0))
    sums = [jnp.zeros(back.shape[1:], F32) for _ in range(2)]
    for k, sender in enumerate(order):
        upper = sender // 4 >= far // 2
        sums[upper] = sums[upper] + back[k]
    left = lane < rows // 2
    dscore = jnp.where(left, sums[0], sums[1])
    outer = jnp.where(left, sums[1], sums[0])
    grads = add_thirds(dot_nt(thirds(scaled[...] * dscore), hits[...]))
    split = row_out.shape[0]
    row_out[...] = grads[:split]
    col_out[...] = grads[split:]
    r, s = iota((RANK, RANK), 0), iota((RANK, RANK), 1)
    result = jnp.zeros((RANK, RANK), F32)
    for k in range(RANK * RANK):
        place_in = lane % (rows // 2)
        mask = jnp.logical_or(place_in == OUTER + k, place_in == OUTER_REST + k)
        value = jnp.sum(jnp.where(mask, outer, 0.0), axis=1, keepdims=True)
        result = jnp.where(r * RANK + s == k, value, result)
    core_out[...] = result


VMEM = pl.BlockSpec(memory_space=pltpu.VMEM)
HBM = pl.BlockSpec(memory_space=pltpu.HBM)


def call(kernel, name, outs, ins, flops, moved, scratch=(), limit=24):
    return pl.pallas_call(
        kernel,
        name=name,
        out_shape=outs,
        in_specs=ins,
        out_specs=jax.tree.map(lambda _: VMEM, outs),
        scratch_shapes=scratch,
        cost_estimate=pl.CostEstimate(flops=flops, bytes_accessed=moved, transcendentals=0),
        compiler_params=pltpu.CompilerParams(vmem_limit_bytes=limit << 20),
    )


def shape(dims, kind):
    return jax.ShapeDtypeStruct(dims, kind)


def local_pairs(grads, values, expand_weight, row_factors, col_factors, core, pair_index, counts):
    far = lax.axis_size("far")
    nmem = 2 * far
    tokens, depth = grads.shape
    vrows, width = values.shape
    rows = pair_index.shape[1]
    factors = NR * RANK + NC * RANK
    swap = [(0, 1), (1, 0)]

    def along_far(block, k):
        return lax.ppermute(block, "far", [(i, i ^ k) for i in range(far)])

    near_weight = lax.ppermute(expand_weight, "near", swap)
    blocks = [shape(((4 if k < WHOLE else 2) * rows + RECORD, 128), BF16) for k in range(far)]
    operands = (pair_index, counts.reshape(1, nmem), core, row_factors.T, col_factors.T, grads)
    *sends, scaled, hits = call(
        functools.partial(prepare_kernel, far),
        "prepare",
        (*blocks, shape((factors, rows), F32), shape((tokens, rows), BF16)),
        [HBM] * 6,
        rows * tokens * depth,
        2 * tokens * depth,
        [pltpu.VMEM(a.shape, a.dtype) for a in operands] + [pltpu.SemaphoreType.DMA((6,))],
    )(*(pltpu.with_memory_space_constraint(a, pltpu.HBM) for a in operands))
    got = {k: along_far(sends[k], k) for k in reversed(range(1, far))}
    ours = [sends[0]] + [got[k] for k in range(1, far)]
    theirs = [lax.ppermute(block, "col", swap) for block in ours[WHOLE:]]
    near_values = lax.ppermute(values, "near", swap)
    code = shape((2 * rows + RECORD, 128), jnp.int16)
    whole, *coded = call(
        functools.partial(project_kernel, far),
        "project",
        (shape((rows, width), F32),) + (code,) * (far - 1),
        [VMEM] * (2 * far - WHOLE + 2),
        4 * E * far * rows * depth // far * width,
        8 * E * width * depth // nmem,
    )(*ours, *theirs, expand_weight, near_weight)
    coded = [along_far(coded[j - 1], j) for j in reversed(range(1, far))]
    fetched, records, value_rows = call(
        functools.partial(lookup_kernel, far),
        "lookup",
        (shape((rows, width), F32), shape((rows, rows), F32), shape((8, rows), F32)),
        [VMEM] * (far + 2),
        2 * rows * vrows * width,
        4 * vrows * width,
    )(*ours, values, near_values)
    fars = sorted(range(far), key=lambda z: abs(2 * z - far))
    contrib, pass_on, back = call(
        functools.partial(reduce_kernel, far, fars),
        "reduce",
        (
            shape((rows // 2, width), BF16),
            shape((rows // 2 + RECORD, width), BF16),
            shape((2 * nmem, 1, rows), F32),
        ),
        [VMEM] * (3 + far),
        8 * rows * width,
        10 * rows * width,
    )(whole, fetched, records, value_rows, *coded)
    order = [4 * z + k for z in fars for k in (3, 2, 1, 0)]
    back = lax.all_to_all(
        back,
        ("far", "near", "col"),
        split_axis=0,
        concat_axis=0,
        axis_index_groups=[order],
        tiled=True,
    )
    passed = lax.ppermute(pass_on, "near", swap)
    value_grad, row_grad, col_grad, core_grad = call(
        functools.partial(output_kernel, far, order),
        "outputs",
        (
            shape((vrows, width), F32),
            shape((NR * RANK, tokens), F32),
            shape((NC * RANK, tokens), F32),
            shape((RANK, RANK), F32),
        ),
        [VMEM] * 6,
        2 * rows * vrows * width,
        4 * vrows * width,
    )(contrib, passed, value_rows, back, scaled, hits)
    return value_grad, row_grad.T, col_grad.T, core_grad


def solution(mesh):
    ngroup, nmem, ncol = (mesh.shape[a] for a in ("group", "mem", "col"))

    def run(*args):
        rows = args[6].shape[1] // (ngroup * nmem)
        depth = args[0].shape[1]
        fits = nmem % 2 == 0 and ncol == 2 and rows == 16 * nmem == 128
        fits = fits and depth == 256 * nmem and args[1].shape[1] == 256 * ncol
        if fits and nmem * rows <= E * depth:
            used = Mesh(
                mesh.devices.reshape(ngroup, nmem // 2, 2, ncol), ("group", "far", "near", "col")
            )
            mem, body = ("far", "near"), local_pairs
        else:
            used, mem, body = mesh, ("mem",), local_weights
        both = ("group",) + mem
        return jax.shard_map(
            body,
            mesh=used,
            in_specs=(
                P(both, None),
                P(mem, "col"),
                P(None, "col", mem),
                P(both, None),
                P(both, None),
                P(),
                P(None, both),
                P(both),
            ),
            out_specs=(
                P(both, "col"),
                P(both, None),
                P(both, None),
                P("group", None),
            ),
            check_vma=False,
        )(*args)

    return run
```

```python
import functools
import math

import jax
import jax.numpy as jnp
from jax import lax
from jax.experimental import pallas as pl
from jax.experimental.pallas import tpu as pltpu
from jax.sharding import Mesh
from jax.sharding import PartitionSpec as P

E = 4
RANK = 2
NR = 8
NC = 8
KC = 64
F32 = jnp.float32
BF16 = jnp.bfloat16

SCORE, ROW_HIGH, ROW_LOW, OUTER, OUTER_REST = 0, 1, 2, 4, 12
RECORD = 16
FULL = 32000.0
WHOLE = 2


def local_weights(grads, values, expand_weight, row_factors, col_factors, core, pair_index, counts):
    nmem = lax.axis_size("mem")
    tokens = grads.shape[0]
    width = values.shape[1]
    vrows = values.shape[0]
    rows = pair_index.shape[1]
    cap = rows // nmem
    high = lax.Precision.HIGHEST
    expanded = jnp.einsum(
        "tn,evn->tev",
        grads,
        lax.all_gather(expand_weight, "mem", axis=2, tiled=True),
        preferred_element_type=jnp.float32,
    ).astype(jnp.bfloat16)
    code = pair_index[0]
    local_row = pair_index[1]
    within = jnp.tile(jnp.arange(cap, dtype=jnp.int32), nmem)
    owner = jnp.repeat(jnp.arange(nmem, dtype=jnp.int32), cap)
    live = within < counts[owner]
    token = code // (NR * NC)
    row_cand = code // NC % NR
    col_cand = code % NC
    a_p = row_factors.reshape(tokens, NR, RANK)[token, row_cand]
    b_p = col_factors.reshape(tokens, NC, RANK)[token, col_cand]
    core_b = jnp.dot(b_p, core.T, precision=high)
    core_a = jnp.dot(a_p, core, precision=high)
    score = jnp.where(live, jnp.sum(a_p * core_b, -1), 0.0).astype(jnp.bfloat16)
    proj = local_row % KC % E
    pair_grad = jnp.where(live[:, None], expanded[token, proj], jnp.zeros((), jnp.bfloat16))
    got_row = lax.all_to_all(
        local_row.reshape(nmem, cap), "mem", split_axis=0, concat_axis=0, tiled=True
    ).reshape(rows)
    fetched = lax.all_to_all(
        values[got_row].reshape(nmem, cap, width), "mem", split_axis=0, concat_axis=0, tiled=True
    ).reshape(rows, width)
    own_contrib = (score.astype(jnp.float32)[:, None] * pair_grad.astype(jnp.float32)).astype(
        jnp.bfloat16
    )
    contrib = lax.all_to_all(
        own_contrib.reshape(nmem, cap, width), "mem", split_axis=0, concat_axis=0, tiled=True
    ).reshape(rows, width)
    dscore = jnp.einsum("pv,pv->p", pair_grad, fetched, preferred_element_type=jnp.float32)
    block = min(2048, rows)

    def add_block(step, total):
        onehot = (jnp.arange(vrows, dtype=jnp.int32)[:, None] == got_row[None, :]).astype(
            jnp.bfloat16
        )
        return total + jnp.dot(onehot, contrib, preferred_element_type=jnp.float32)

    value_grad = lax.fori_loop(0, rows // block, add_block, jnp.zeros((vrows, width), jnp.float32))
    dscore = lax.psum(dscore, "col")
    row_grad = jax.ops.segment_sum(
        dscore[:, None] * core_b, token * NR + row_cand, num_segments=tokens * NR
    )
    col_grad = jax.ops.segment_sum(
        dscore[:, None] * core_a, token * NC + col_cand, num_segments=tokens * NC
    )
    row_grad = row_grad.reshape(tokens, NR * RANK)
    col_grad = col_grad.reshape(tokens, NC * RANK)
    core_part = jnp.dot((dscore[:, None] * a_p).T, b_p, precision=high)
    core_grad = lax.psum(core_part, "mem")
    return (value_grad, row_grad, col_grad, core_grad)


def iota(shape, dim):
    return lax.broadcasted_iota(jnp.int32, shape, dim)


def dot_nn(x, y):
    return jnp.dot(x, y, preferred_element_type=F32)


def dot_nt(x, y):
    return lax.dot_general(x, y, (((1,), (1,)), ((), ())), preferred_element_type=F32)


def thirds(x):
    first = x.astype(BF16)
    rest = x - first.astype(F32)
    second = rest.astype(BF16)
    third = (rest - second.astype(F32)).astype(BF16)
    return jnp.concatenate([first, second, third], axis=0)


def add_thirds(y):
    n = y.shape[0] // 3
    return (y[2 * n :] + y[n : 2 * n]) + y[:n]


def place():
    return lax.axis_index("far"), lax.axis_index("near"), lax.axis_index("col")


def prepare_kernel(far, *refs):
    sources, sends, (scaled, hits, *targets, sems) = refs[:6], refs[6 : 6 + far], refs[6 + far :]
    pair, counts, core, row_fac, col_fac, grads = targets
    copies = [
        pltpu.make_async_copy(source, target, sems.at[k])
        for k, (source, target) in enumerate(zip(sources, targets))
    ]
    for copy in copies:
        copy.start()
    for copy in copies[:-1]:
        copy.wait()
    z, x, c = place()
    nmem = 2 * far
    rows = pair.shape[1]
    cap = rows // nmem
    half = cap // 2
    tokens, depth = grads.shape
    shard = depth // nmem
    code = pair[0:1, :]
    local_row = pair[1:2, :]
    lane = iota((1, rows), 1)
    owner = lane // cap
    limit = jnp.zeros((1, rows), jnp.int32)
    for o in range(nmem):
        limit = jnp.where(owner == o, counts[0:1, o : o + 1], limit)
    live = lane % cap < limit
    token = code // (NR * NC)
    row_cand = code // NC % NR
    col_cand = code % NC
    hit = iota((tokens, rows), 0) == token
    hot = jnp.where(hit, 1.0, 0.0).astype(BF16)
    factors = jnp.concatenate([row_fac[...], col_fac[...]], axis=0)
    found = add_thirds(dot_nn(thirds(factors), hot))
    at = iota(found.shape, 0)
    split = NR * RANK

    def pick(row):
        return jnp.sum(jnp.where(at == row, found, 0.0), axis=0, keepdims=True)

    a0, a1 = pick(row_cand * RANK), pick(row_cand * RANK + 1)
    b0, b1 = pick(split + col_cand * RANK), pick(split + col_cand * RANK + 1)
    c00, c01, c10, c11 = core[0:1, 0:1], core[0:1, 1:2], core[1:2, 0:1], core[1:2, 1:2]
    core_b0, core_b1 = c00 * b0 + c01 * b1, c10 * b0 + c11 * b1
    score = jnp.where(live, a0 * core_b0 + a1 * core_b1, 0.0)
    hits[...] = hot
    core_a0, core_a1 = c00 * a0 + c10 * a1, c01 * a0 + c11 * a1
    even = at % RANK == 0
    of_row = jnp.where(at // RANK == row_cand, jnp.where(even, core_b0, core_b1), 0.0)
    of_col = jnp.where((at - split) // RANK == col_cand, jnp.where(even, core_a0, core_a1), 0.0)
    scaled[...] = jnp.where(at < split, of_row, of_col)

    field = iota((RECORD, rows), 0)
    record = jnp.where(field == SCORE, score, 0.0)
    record = jnp.where(field == ROW_HIGH, (local_row // KC).astype(F32), record)
    record = jnp.where(field == ROW_LOW, (local_row % KC).astype(F32), record)
    for k, outer in enumerate((a0 * b0, a0 * b1, a1 * b0, a1 * b1)):
        top = outer.astype(BF16).astype(F32)
        record = jnp.where(field == OUTER + k, top, record)
        record = jnp.where(field == OUTER_REST + k, outer - top, record)

    to = iota((rows, rows), 1)
    to_m, to_y = to // (2 * cap), to // cap % 2
    to_pair = ((to_m ^ z) * 2 + (to_y ^ x)) * cap + (to // half % 2 ^ c) * half + to % half
    order = jnp.where(iota((rows, rows), 0) == to_pair, 1.0, 0.0).astype(BF16)
    records = dot_nn(record.astype(BF16), order).astype(BF16)

    q = iota((rows, rows), 0)
    mine = rows // 2
    q_pair = ((q % mine // cap ^ z) * 2 + (q // half % 2 ^ x)) * cap
    q_pair = q_pair + (q // mine ^ c) * half + q % half
    take = jnp.where(iota((rows, rows), 1) == q_pair, 1.0, 0.0).astype(BF16)
    live_hits = jnp.where(jnp.logical_and(hit, live), 1.0, 0.0).astype(BF16)
    chosen = dot_nt(take, live_hits).astype(BF16)
    copies[-1].wait()
    for k in range(far):
        taken = []
        for y in range(2):
            start = pl.multiple_of(((z ^ k) * 2 + (x ^ y)) * shard, shard)
            part = grads[:, pl.ds(start, shard)]
            taken.append(dot_nn(chosen if k < WHOLE else chosen[:mine], part).astype(BF16))
        blocks = []
        for g in range(2 if k < WHOLE else 1):
            for part in taken:
                part = part[g * mine : (g + 1) * mine]
                blocks += [part[:, :128], part[:, 128:]]
        sends[k][...] = jnp.concatenate(blocks + [records], axis=0)


def project_kernel(far, *refs):
    ours, theirs = refs[:far], refs[far : 2 * far - WHOLE]
    own, near, whole, *coded = refs[2 * far - WHOLE :]
    mine = (ours[far - 1].shape[0] - RECORD) // 4
    cap = mine // far // 2 * 2
    half = cap // 2
    rows = 2 * mine
    lane, line = iota((rows, rows), 1), iota((rows, rows), 0)
    mask = line % mine // half * cap + line // mine * half + line % half == lane
    firsts, seconds, projs = [], [], []
    for k in range(far):
        for g in range(2):
            block, at = (ours[k], 4 * mine * g) if k < WHOLE or g == 0 else (theirs[k - WHOLE], 0)
            quarters = [block[at + i * mine : at + (i + 1) * mine] for i in range(4)]
            firsts.append(jnp.concatenate(quarters[:2], axis=1))
            seconds.append(jnp.concatenate(quarters[2:], axis=1))
        at = ours[k].shape[0] - RECORD
        record = ours[k][at : at + RECORD].astype(F32)
        low = jnp.where(mask, record[ROW_LOW : ROW_LOW + 1], 0.0)
        projs.append(jnp.sum(low, axis=1, keepdims=True))
    first, second = jnp.concatenate(firsts, axis=0), jnp.concatenate(seconds, axis=0)
    proj = jnp.concatenate(projs, axis=0).astype(jnp.int32) % E
    total = None
    for e in range(E):
        here = dot_nt(first, own[e]) + dot_nt(second, near[e])
        total = here if total is None else jnp.where(proj == e, here, total)

    def rows_for(j):
        pieces = []
        for y in range(2):
            for n in range(far):
                for g in range(2):
                    start = (j ^ n) * rows + g * mine + n * cap + y * half
                    pieces.append(total[start : start + half])
        return jnp.concatenate(pieces, axis=0)

    whole[...] = rows_for(0)
    diagonal = line == lane
    for j in range(1, far):
        part = rows_for(j)
        top = jnp.max(jnp.abs(part), axis=1, keepdims=True)
        power = jnp.floor(jnp.log(jnp.maximum(top, 2.0**-126)) * (1 / math.log(2))) + 1.0
        level = jnp.abs(part) * jnp.exp2(-power)
        root = level * lax.rsqrt(jnp.maximum(level, 1e-30)) * FULL
        code = jnp.floor(jnp.where(part < 0, -root, root) + 0.5)
        powers = jnp.sum(jnp.where(diagonal, power, 0.0), axis=0, keepdims=True)
        powers = jnp.broadcast_to(powers, (RECORD, rows))
        block = jnp.concatenate([code[:, :128], code[:, 128:], powers], axis=0)
        coded[j - 1][...] = block.astype(jnp.int32).astype(jnp.int16)


def lookup_kernel(far, *refs):
    blocks, (values, near_values), (fetched, records, value_rows) = (
        refs[:far],
        refs[far : far + 2],
        refs[far + 2 :],
    )
    rows = records.shape[0]
    group = rows // far
    lane, line = iota((rows, rows), 1), iota((rows, rows), 0)
    total = jnp.zeros((RECORD, rows), F32)
    for n in range(far):
        at = blocks[n].shape[0] - RECORD
        tile = blocks[n][at : at + RECORD]
        source = n * group + lane // (rows // 2) * (group // 2) + lane % (group // 2)
        inside = lane // (group // 2) % far == n
        move = jnp.where(jnp.logical_and(line == source, inside), 1.0, 0.0).astype(BF16)
        total = total + dot_nn(tile, move)
    value_row = KC * total[ROW_HIGH : ROW_HIGH + 1] + total[ROW_LOW : ROW_LOW + 1]
    value_rows[...] = jnp.broadcast_to(value_row, value_rows.shape)
    padded = jnp.concatenate([total, jnp.zeros((rows - RECORD, rows), F32)], axis=0).astype(BF16)
    column = dot_nt(jnp.where(line == lane, 1.0, 0.0).astype(BF16), padded)
    records[...] = column
    row = KC * column[:, ROW_HIGH : ROW_HIGH + 1] + column[:, ROW_LOW : ROW_LOW + 1]
    hot = iota((rows, values.shape[0]), 1) == row.astype(jnp.int32)
    hot = jnp.where(hot, 1.0, 0.0).astype(BF16)
    fetched[: rows // 2] = dot_nn(hot[: rows // 2], values[...])
    fetched[rows // 2 :] = dot_nn(hot[rows // 2 :], near_values[...])


def reduce_kernel(far, fars, *refs):
    (whole, fetched, records, value_rows), coded, (contrib, pass_on, back) = (
        refs[:4],
        refs[4 : 3 + far],
        refs[3 + far :],
    )
    z, x, c = place()
    rows, width = whole.shape
    half = rows // far // 4
    line, lane = iota((rows, rows), 0), iota((rows, rows), 1)
    diagonal = line == lane
    total = whole[...]
    for block in coded:
        code = block[...].astype(jnp.int32).astype(F32)
        power = jnp.where(diagonal, code[2 * rows : 2 * rows + 1], 0.0)
        scale = jnp.exp2(jnp.sum(power, axis=1, keepdims=True))
        value = jnp.concatenate([code[:rows], code[rows : 2 * rows]], axis=1) * (1 / FULL)
        total = total + value * jnp.abs(value) * scale
    pair_grad = total.astype(BF16).astype(F32)
    record = records[...]
    share = record[:, SCORE : SCORE + 1] * pair_grad
    contrib[...] = share[: rows // 2].astype(BF16)
    send = value_rows[0:1]
    send_high = jnp.floor(send * (1 / KC))
    tile = iota((RECORD, width), 0)
    spare = jnp.zeros((1, width - rows), F32)
    high_row = jnp.concatenate([send_high, spare], axis=1)
    low_row = jnp.concatenate([send - KC * send_high, spare], axis=1)
    tail = jnp.where(tile == 0, high_row, jnp.where(tile == 1, low_row, 0.0))
    pass_on[...] = jnp.concatenate([share[rows // 2 :], tail], axis=0).astype(BF16)
    dscore = jnp.sum(pair_grad * fetched[...], axis=1, keepdims=True)
    owner = z * 2 + (line // (rows // 2) ^ x)
    target = owner * (2 * half) + (line // half % 2 ^ c) * half + line % half
    spread = jnp.where(lane == target, dscore, 0.0).reshape(2, far, 2 * half, rows)
    spread = jnp.sum(spread[0] + spread[1], axis=1)
    outer = jnp.sum(dscore * record, axis=0, keepdims=True)
    low = z < far // 2
    core_row = jnp.where(low, pltpu.roll(outer, rows // 2, 1), outer)
    core_lane = iota((1, rows), 1) - jnp.where(low, rows // 2, 0)
    core_row = jnp.where(jnp.logical_and(core_lane >= 0, core_lane < RECORD), core_row, 0.0)
    for n in range(far):
        for k in range(4):
            row = jnp.where(x == k // 2, spread[n : n + 1], 0.0) + core_row
            rank = sum(jnp.where(z ^ n == far_at, at, 0) for at, far_at in enumerate(fars))
            back[rank * 4 + 3 - k] = row


def output_kernel(far, order, contrib, passed, value_rows, back, scaled, hits, *outs):
    out, row_out, col_out, core_out = outs
    half = contrib.shape[0]
    rows = 2 * half
    tail = passed[half : half + RECORD].astype(F32)
    lane = iota((1, rows), 1)
    other = (KC * tail[0:1] + tail[1:2])[:, :rows]
    row = jnp.where(lane < half, value_rows[0:1], other).astype(jnp.int32)
    hot = jnp.where(iota((out.shape[0], rows), 0) == row, 1.0, 0.0).astype(BF16)
    out[...] = dot_nn(hot, jnp.concatenate([contrib[...], passed[:half]], axis=0))
    sums = [jnp.zeros(back.shape[1:], F32) for _ in range(2)]
    for k, sender in enumerate(order):
        upper = sender // 4 >= far // 2
        sums[upper] = sums[upper] + back[k]
    left = lane < rows // 2
    dscore = jnp.where(left, sums[0], sums[1])
    outer = jnp.where(left, sums[1], sums[0])
    grads = add_thirds(dot_nt(thirds(scaled[...] * dscore), hits[...]))
    split = row_out.shape[0]
    row_out[...] = grads[:split]
    col_out[...] = grads[split:]
    r, s = iota((RANK, RANK), 0), iota((RANK, RANK), 1)
    result = jnp.zeros((RANK, RANK), F32)
    for k in range(RANK * RANK):
        place_in = lane % (rows // 2)
        mask = jnp.logical_or(place_in == OUTER + k, place_in == OUTER_REST + k)
        value = jnp.sum(jnp.where(mask, outer, 0.0), axis=1, keepdims=True)
        result = jnp.where(r * RANK + s == k, value, result)
    core_out[...] = result


VMEM = pl.BlockSpec(memory_space=pltpu.VMEM)
HBM = pl.BlockSpec(memory_space=pltpu.HBM)


def call(kernel, name, outs, ins, flops, moved, scratch=(), limit=24):
    return pl.pallas_call(
        kernel,
        name=name,
        out_shape=outs,
        in_specs=ins,
        out_specs=jax.tree.map(lambda _: VMEM, outs),
        scratch_shapes=scratch,
        cost_estimate=pl.CostEstimate(flops=64 * flops, bytes_accessed=16 * moved, transcendentals=0),
        compiler_params=pltpu.CompilerParams(vmem_limit_bytes=limit << 20),
    )


def shape(dims, kind):
    return jax.ShapeDtypeStruct(dims, kind)


def local_pairs(grads, values, expand_weight, row_factors, col_factors, core, pair_index, counts):
    far = lax.axis_size("far")
    nmem = 2 * far
    tokens, depth = grads.shape
    vrows, width = values.shape
    rows = pair_index.shape[1]
    factors = NR * RANK + NC * RANK
    swap = [(0, 1), (1, 0)]

    def along_far(block, k):
        return lax.ppermute(block, "far", [(i, i ^ k) for i in range(far)])

    near_weight = lax.ppermute(expand_weight, "near", swap)
    blocks = [shape(((4 if k < WHOLE else 2) * rows + RECORD, 128), BF16) for k in range(far)]
    operands = (pair_index, counts.reshape(1, nmem), core, row_factors.T, col_factors.T, grads)
    *sends, scaled, hits = call(
        functools.partial(prepare_kernel, far),
        "prepare",
        (*blocks, shape((factors, rows), F32), shape((tokens, rows), BF16)),
        [HBM] * 6,
        rows * tokens * depth,
        2 * tokens * depth,
        [pltpu.VMEM(a.shape, a.dtype) for a in operands] + [pltpu.SemaphoreType.DMA((6,))],
    )(*(pltpu.with_memory_space_constraint(a, pltpu.HBM) for a in operands))
    got = {k: along_far(sends[k], k) for k in reversed(range(1, far))}
    ours = [sends[0]] + [got[k] for k in range(1, far)]
    theirs = [lax.ppermute(block, "col", swap) for block in ours[WHOLE:]]
    near_values = lax.ppermute(values, "near", swap)
    code = shape((2 * rows + RECORD, 128), jnp.int16)
    whole, *coded = call(
        functools.partial(project_kernel, far),
        "project",
        (shape((rows, width), F32),) + (code,) * (far - 1),
        [VMEM] * (2 * far - WHOLE + 2),
        4 * E * far * rows * depth // far * width,
        8 * E * width * depth // nmem,
    )(*ours, *theirs, expand_weight, near_weight)
    coded = [along_far(coded[j - 1], j) for j in reversed(range(1, far))]
    fetched, records, value_rows = call(
        functools.partial(lookup_kernel, far),
        "lookup",
        (shape((rows, width), F32), shape((rows, rows), F32), shape((8, rows), F32)),
        [VMEM] * (far + 2),
        2 * rows * vrows * width,
        4 * vrows * width,
    )(*ours, values, near_values)
    fars = sorted(range(far), key=lambda z: abs(2 * z - far))
    contrib, pass_on, back = call(
        functools.partial(reduce_kernel, far, fars),
        "reduce",
        (
            shape((rows // 2, width), BF16),
            shape((rows // 2 + RECORD, width), BF16),
            shape((2 * nmem, 1, rows), F32),
        ),
        [VMEM] * (3 + far),
        8 * rows * width,
        10 * rows * width,
    )(whole, fetched, records, value_rows, *coded)
    order = [4 * z + k for z in fars for k in (3, 2, 1, 0)]
    back = lax.all_to_all(
        back,
        ("far", "near", "col"),
        split_axis=0,
        concat_axis=0,
        axis_index_groups=[order],
        tiled=True,
    )
    passed = lax.ppermute(pass_on, "near", swap)
    value_grad, row_grad, col_grad, core_grad = call(
        functools.partial(output_kernel, far, order),
        "outputs",
        (
            shape((vrows, width), F32),
            shape((NR * RANK, tokens), F32),
            shape((NC * RANK, tokens), F32),
            shape((RANK, RANK), F32),
        ),
        [VMEM] * 6,
        2 * rows * vrows * width,
        4 * vrows * width,
    )(contrib, passed, value_rows, back, scaled, hits)
    return value_grad, row_grad.T, col_grad.T, core_grad


def solution(mesh):
    ngroup, nmem, ncol = (mesh.shape[a] for a in ("group", "mem", "col"))

    def run(*args):
        rows = args[6].shape[1] // (ngroup * nmem)
        depth = args[0].shape[1]
        fits = nmem % 2 == 0 and ncol == 2 and rows == 16 * nmem == 128
        fits = fits and depth == 256 * nmem and args[1].shape[1] == 256 * ncol
        if fits and nmem * rows <= E * depth:
            used = Mesh(
                mesh.devices.reshape(ngroup, nmem // 2, 2, ncol), ("group", "far", "near", "col")
            )
            mem, body = ("far", "near"), local_pairs
        else:
            used, mem, body = mesh, ("mem",), local_weights
        both = ("group",) + mem
        return jax.shard_map(
            body,
            mesh=used,
            in_specs=(
                P(both, None),
                P(mem, "col"),
                P(None, "col", mem),
                P(both, None),
                P(both, None),
                P(),
                P(None, both),
                P(both),
            ),
            out_specs=(
                P(both, "col"),
                P(both, None),
                P(both, None),
                P("group", None),
            ),
            check_vma=False,
        )(*args)

    return run
```

```python
import functools
import math

import jax
import jax.numpy as jnp
from jax import lax
from jax.experimental import pallas as pl
from jax.experimental.pallas import tpu as pltpu
from jax.sharding import Mesh
from jax.sharding import PartitionSpec as P

E = 4
RANK = 2
NR = 8
NC = 8
KC = 64
F32 = jnp.float32
BF16 = jnp.bfloat16

SCORE, ROW_HIGH, ROW_LOW, OUTER, OUTER_REST = 0, 1, 2, 4, 12
RECORD = 16
FULL = 32000.0
WHOLE = 2


def local_weights(grads, values, expand_weight, row_factors, col_factors, core, pair_index, counts):
    nmem = lax.axis_size("mem")
    tokens = grads.shape[0]
    width = values.shape[1]
    vrows = values.shape[0]
    rows = pair_index.shape[1]
    cap = rows // nmem
    high = lax.Precision.HIGHEST
    expanded = jnp.einsum(
        "tn,evn->tev",
        grads,
        lax.all_gather(expand_weight, "mem", axis=2, tiled=True),
        preferred_element_type=jnp.float32,
    ).astype(jnp.bfloat16)
    code = pair_index[0]
    local_row = pair_index[1]
    within = jnp.tile(jnp.arange(cap, dtype=jnp.int32), nmem)
    owner = jnp.repeat(jnp.arange(nmem, dtype=jnp.int32), cap)
    live = within < counts[owner]
    token = code // (NR * NC)
    row_cand = code // NC % NR
    col_cand = code % NC
    a_p = row_factors.reshape(tokens, NR, RANK)[token, row_cand]
    b_p = col_factors.reshape(tokens, NC, RANK)[token, col_cand]
    core_b = jnp.dot(b_p, core.T, precision=high)
    core_a = jnp.dot(a_p, core, precision=high)
    score = jnp.where(live, jnp.sum(a_p * core_b, -1), 0.0).astype(jnp.bfloat16)
    proj = local_row % KC % E
    pair_grad = jnp.where(live[:, None], expanded[token, proj], jnp.zeros((), jnp.bfloat16))
    got_row = lax.all_to_all(
        local_row.reshape(nmem, cap), "mem", split_axis=0, concat_axis=0, tiled=True
    ).reshape(rows)
    fetched = lax.all_to_all(
        values[got_row].reshape(nmem, cap, width), "mem", split_axis=0, concat_axis=0, tiled=True
    ).reshape(rows, width)
    own_contrib = (score.astype(jnp.float32)[:, None] * pair_grad.astype(jnp.float32)).astype(
        jnp.bfloat16
    )
    contrib = lax.all_to_all(
        own_contrib.reshape(nmem, cap, width), "mem", split_axis=0, concat_axis=0, tiled=True
    ).reshape(rows, width)
    dscore = jnp.einsum("pv,pv->p", pair_grad, fetched, preferred_element_type=jnp.float32)
    block = min(2048, rows)

    def add_block(step, total):
        onehot = (jnp.arange(vrows, dtype=jnp.int32)[:, None] == got_row[None, :]).astype(
            jnp.bfloat16
        )
        return total + jnp.dot(onehot, contrib, preferred_element_type=jnp.float32)

    value_grad = lax.fori_loop(0, rows // block, add_block, jnp.zeros((vrows, width), jnp.float32))
    dscore = lax.psum(dscore, "col")
    row_grad = jax.ops.segment_sum(
        dscore[:, None] * core_b, token * NR + row_cand, num_segments=tokens * NR
    )
    col_grad = jax.ops.segment_sum(
        dscore[:, None] * core_a, token * NC + col_cand, num_segments=tokens * NC
    )
    row_grad = row_grad.reshape(tokens, NR * RANK)
    col_grad = col_grad.reshape(tokens, NC * RANK)
    core_part = jnp.dot((dscore[:, None] * a_p).T, b_p, precision=high)
    core_grad = lax.psum(core_part, "mem")
    return (value_grad, row_grad, col_grad, core_grad)


def iota(shape, dim):
    return lax.broadcasted_iota(jnp.int32, shape, dim)


def dot_nn(x, y):
    return jnp.dot(x, y, preferred_element_type=F32)


def dot_nt(x, y):
    return lax.dot_general(x, y, (((1,), (1,)), ((), ())), preferred_element_type=F32)


def thirds(x):
    first = x.astype(BF16)
    rest = x - first.astype(F32)
    second = rest.astype(BF16)
    third = (rest - second.astype(F32)).astype(BF16)
    return jnp.concatenate([first, second, third], axis=0)


def add_thirds(y):
    n = y.shape[0] // 3
    return (y[2 * n :] + y[n : 2 * n]) + y[:n]


def place():
    return lax.axis_index("far"), lax.axis_index("near"), lax.axis_index("col")


def prepare_kernel(far, *refs):
    sources, sends, (scaled, hits, *targets, sems) = refs[:6], refs[6 : 6 + far], refs[6 + far :]
    pair, counts, core, row_fac, col_fac, grads = targets
    copies = [
        pltpu.make_async_copy(source, target, sems.at[k])
        for k, (source, target) in enumerate(zip(sources, targets))
    ]
    for copy in copies:
        copy.start()
    for copy in copies[:-1]:
        copy.wait()
    z, x, c = place()
    nmem = 2 * far
    rows = pair.shape[1]
    cap = rows // nmem
    half = cap // 2
    tokens, depth = grads.shape
    shard = depth // nmem
    code = pair[0:1, :]
    local_row = pair[1:2, :]
    lane = iota((1, rows), 1)
    owner = lane // cap
    limit = jnp.zeros((1, rows), jnp.int32)
    for o in range(nmem):
        limit = jnp.where(owner == o, counts[0:1, o : o + 1], limit)
    live = lane % cap < limit
    token = code // (NR * NC)
    row_cand = code // NC % NR
    col_cand = code % NC
    hit = iota((tokens, rows), 0) == token
    hot = jnp.where(hit, 1.0, 0.0).astype(BF16)
    factors = jnp.concatenate([row_fac[...], col_fac[...]], axis=0)
    found = add_thirds(dot_nn(thirds(factors), hot))
    at = iota(found.shape, 0)
    split = NR * RANK

    def pick(row):
        return jnp.sum(jnp.where(at == row, found, 0.0), axis=0, keepdims=True)

    a0, a1 = pick(row_cand * RANK), pick(row_cand * RANK + 1)
    b0, b1 = pick(split + col_cand * RANK), pick(split + col_cand * RANK + 1)
    c00, c01, c10, c11 = core[0:1, 0:1], core[0:1, 1:2], core[1:2, 0:1], core[1:2, 1:2]
    core_b0, core_b1 = c00 * b0 + c01 * b1, c10 * b0 + c11 * b1
    score = jnp.where(live, a0 * core_b0 + a1 * core_b1, 0.0)
    hits[...] = hot
    core_a0, core_a1 = c00 * a0 + c10 * a1, c01 * a0 + c11 * a1
    even = at % RANK == 0
    of_row = jnp.where(at // RANK == row_cand, jnp.where(even, core_b0, core_b1), 0.0)
    of_col = jnp.where((at - split) // RANK == col_cand, jnp.where(even, core_a0, core_a1), 0.0)
    scaled[...] = jnp.where(at < split, of_row, of_col)

    field = iota((RECORD, rows), 0)
    record = jnp.where(field == SCORE, score, 0.0)
    record = jnp.where(field == ROW_HIGH, (local_row // KC).astype(F32), record)
    record = jnp.where(field == ROW_LOW, (local_row % KC).astype(F32), record)
    for k, outer in enumerate((a0 * b0, a0 * b1, a1 * b0, a1 * b1)):
        top = outer.astype(BF16).astype(F32)
        record = jnp.where(field == OUTER + k, top, record)
        record = jnp.where(field == OUTER_REST + k, outer - top, record)

    to = iota((rows, rows), 1)
    to_m, to_y = to // (2 * cap), to // cap % 2
    to_pair = ((to_m ^ z) * 2 + (to_y ^ x)) * cap + (to // half % 2 ^ c) * half + to % half
    order = jnp.where(iota((rows, rows), 0) == to_pair, 1.0, 0.0).astype(BF16)
    records = dot_nn(record.astype(BF16), order).astype(BF16)

    q = iota((rows, rows), 0)
    mine = rows // 2
    q_pair = ((q % mine // cap ^ z) * 2 + (q // half % 2 ^ x)) * cap
    q_pair = q_pair + (q // mine ^ c) * half + q % half
    take = jnp.where(iota((rows, rows), 1) == q_pair, 1.0, 0.0).astype(BF16)
    live_hits = jnp.where(jnp.logical_and(hit, live), 1.0, 0.0).astype(BF16)
    chosen = dot_nt(take, live_hits).astype(BF16)
    copies[-1].wait()
    for k in range(far):
        taken = []
        for y in range(2):
            start = pl.multiple_of(((z ^ k) * 2 + (x ^ y)) * shard, shard)
            part = grads[:, pl.ds(start, shard)]
            taken.append(dot_nn(chosen if k < WHOLE else chosen[:mine], part).astype(BF16))
        blocks = []
        for g in range(2 if k < WHOLE else 1):
            for part in taken:
                part = part[g * mine : (g + 1) * mine]
                blocks += [part[:, :128], part[:, 128:]]
        sends[k][...] = jnp.concatenate(blocks + [records], axis=0)


def project_kernel(far, *refs):
    ours, theirs = refs[:far], refs[far : 2 * far - WHOLE]
    own, near, whole, *coded = refs[2 * far - WHOLE :]
    mine = (ours[far - 1].shape[0] - RECORD) // 4
    cap = mine // far // 2 * 2
    half = cap // 2
    rows = 2 * mine
    lane, line = iota((rows, rows), 1), iota((rows, rows), 0)
    mask = line % mine // half * cap + line // mine * half + line % half == lane
    firsts, seconds, projs = [], [], []
    for k in range(far):
        for g in range(2):
            block, at = (ours[k], 4 * mine * g) if k < WHOLE or g == 0 else (theirs[k - WHOLE], 0)
            quarters = [block[at + i * mine : at + (i + 1) * mine] for i in range(4)]
            firsts.append(jnp.concatenate(quarters[:2], axis=1))
            seconds.append(jnp.concatenate(quarters[2:], axis=1))
        at = ours[k].shape[0] - RECORD
        record = ours[k][at : at + RECORD].astype(F32)
        low = jnp.where(mask, record[ROW_LOW : ROW_LOW + 1], 0.0)
        projs.append(jnp.sum(low, axis=1, keepdims=True))
    first, second = jnp.concatenate(firsts, axis=0), jnp.concatenate(seconds, axis=0)
    proj = jnp.concatenate(projs, axis=0).astype(jnp.int32) % E
    total = None
    for e in range(E):
        here = dot_nt(first, own[e]) + dot_nt(second, near[e])
        total = here if total is None else jnp.where(proj == e, here, total)

    def rows_for(j):
        pieces = []
        for y in range(2):
            for n in range(far):
                for g in range(2):
                    start = (j ^ n) * rows + g * mine + n * cap + y * half
                    pieces.append(total[start : start + half])
        return jnp.concatenate(pieces, axis=0)

    whole[...] = rows_for(0)
    diagonal = line == lane
    for j in range(1, far):
        part = rows_for(j)
        top = jnp.max(jnp.abs(part), axis=1, keepdims=True)
        power = jnp.floor(jnp.log(jnp.maximum(top, 2.0**-126)) * (1 / math.log(2))) + 1.0
        level = jnp.abs(part) * jnp.exp2(-power)
        root = level * lax.rsqrt(jnp.maximum(level, 1e-30)) * FULL
        code = jnp.floor(jnp.where(part < 0, -root, root) + 0.5)
        powers = jnp.sum(jnp.where(diagonal, power, 0.0), axis=0, keepdims=True)
        powers = jnp.broadcast_to(powers, (RECORD, rows))
        block = jnp.concatenate([code[:, :128], code[:, 128:], powers], axis=0)
        coded[j - 1][...] = block.astype(jnp.int32).astype(jnp.int16)


def lookup_kernel(far, *refs):
    blocks, (values, near_values), (fetched, records, value_rows) = (
        refs[:far],
        refs[far : far + 2],
        refs[far + 2 :],
    )
    rows = records.shape[0]
    group = rows // far
    lane, line = iota((rows, rows), 1), iota((rows, rows), 0)
    total = jnp.zeros((RECORD, rows), F32)
    for n in range(far):
        at = blocks[n].shape[0] - RECORD
        tile = blocks[n][at : at + RECORD]
        source = n * group + lane // (rows // 2) * (group // 2) + lane % (group // 2)
        inside = lane // (group // 2) % far == n
        move = jnp.where(jnp.logical_and(line == source, inside), 1.0, 0.0).astype(BF16)
        total = total + dot_nn(tile, move)
    value_row = KC * total[ROW_HIGH : ROW_HIGH + 1] + total[ROW_LOW : ROW_LOW + 1]
    value_rows[...] = jnp.broadcast_to(value_row, value_rows.shape)
    padded = jnp.concatenate([total, jnp.zeros((rows - RECORD, rows), F32)], axis=0).astype(BF16)
    column = dot_nt(jnp.where(line == lane, 1.0, 0.0).astype(BF16), padded)
    records[...] = column
    row = KC * column[:, ROW_HIGH : ROW_HIGH + 1] + column[:, ROW_LOW : ROW_LOW + 1]
    hot = iota((rows, values.shape[0]), 1) == row.astype(jnp.int32)
    hot = jnp.where(hot, 1.0, 0.0).astype(BF16)
    fetched[: rows // 2] = dot_nn(hot[: rows // 2], values[...])
    fetched[rows // 2 :] = dot_nn(hot[rows // 2 :], near_values[...])


def reduce_kernel(far, fars, *refs):
    (whole, fetched, records, value_rows), coded, (contrib, pass_on, back) = (
        refs[:4],
        refs[4 : 3 + far],
        refs[3 + far :],
    )
    z, x, c = place()
    rows, width = whole.shape
    half = rows // far // 4
    line, lane = iota((rows, rows), 0), iota((rows, rows), 1)
    diagonal = line == lane
    total = whole[...]
    for block in coded:
        code = block[...].astype(jnp.int32).astype(F32)
        power = jnp.where(diagonal, code[2 * rows : 2 * rows + 1], 0.0)
        scale = jnp.exp2(jnp.sum(power, axis=1, keepdims=True))
        value = jnp.concatenate([code[:rows], code[rows : 2 * rows]], axis=1) * (1 / FULL)
        total = total + value * jnp.abs(value) * scale
    pair_grad = total.astype(BF16).astype(F32)
    record = records[...]
    share = record[:, SCORE : SCORE + 1] * pair_grad
    contrib[...] = share[: rows // 2].astype(BF16)
    send = value_rows[0:1]
    send_high = jnp.floor(send * (1 / KC))
    tile = iota((RECORD, width), 0)
    spare = jnp.zeros((1, width - rows), F32)
    high_row = jnp.concatenate([send_high, spare], axis=1)
    low_row = jnp.concatenate([send - KC * send_high, spare], axis=1)
    tail = jnp.where(tile == 0, high_row, jnp.where(tile == 1, low_row, 0.0))
    pass_on[...] = jnp.concatenate([share[rows // 2 :], tail], axis=0).astype(BF16)
    dscore = jnp.sum(pair_grad * fetched[...], axis=1, keepdims=True)
    owner = z * 2 + (line // (rows // 2) ^ x)
    target = owner * (2 * half) + (line // half % 2 ^ c) * half + line % half
    spread = jnp.where(lane == target, dscore, 0.0).reshape(2, far, 2 * half, rows)
    spread = jnp.sum(spread[0] + spread[1], axis=1)
    outer = jnp.sum(dscore * record, axis=0, keepdims=True)
    low = z < far // 2
    core_row = jnp.where(low, pltpu.roll(outer, rows // 2, 1), outer)
    core_lane = iota((1, rows), 1) - jnp.where(low, rows // 2, 0)
    core_row = jnp.where(jnp.logical_and(core_lane >= 0, core_lane < RECORD), core_row, 0.0)
    for n in range(far):
        for k in range(4):
            row = jnp.where(x == k // 2, spread[n : n + 1], 0.0) + core_row
            rank = sum(jnp.where(z ^ n == far_at, at, 0) for at, far_at in enumerate(fars))
            back[rank * 4 + 3 - k] = row


def output_kernel(far, order, contrib, passed, value_rows, back, scaled, hits, *outs):
    out, row_out, col_out, core_out = outs
    half = contrib.shape[0]
    rows = 2 * half
    tail = passed[half : half + RECORD].astype(F32)
    lane = iota((1, rows), 1)
    other = (KC * tail[0:1] + tail[1:2])[:, :rows]
    row = jnp.where(lane < half, value_rows[0:1], other).astype(jnp.int32)
    hot = jnp.where(iota((out.shape[0], rows), 0) == row, 1.0, 0.0).astype(BF16)
    out[...] = dot_nn(hot, jnp.concatenate([contrib[...], passed[:half]], axis=0))
    sums = [jnp.zeros(back.shape[1:], F32) for _ in range(2)]
    for k, sender in enumerate(order):
        upper = sender // 4 >= far // 2
        sums[upper] = sums[upper] + back[k]
    left = lane < rows // 2
    dscore = jnp.where(left, sums[0], sums[1])
    outer = jnp.where(left, sums[1], sums[0])
    grads = add_thirds(dot_nt(thirds(scaled[...] * dscore), hits[...]))
    split = row_out.shape[0]
    row_out[...] = grads[:split]
    col_out[...] = grads[split:]
    r, s = iota((RANK, RANK), 0), iota((RANK, RANK), 1)
    result = jnp.zeros((RANK, RANK), F32)
    for k in range(RANK * RANK):
        place_in = lane % (rows // 2)
        mask = jnp.logical_or(place_in == OUTER + k, place_in == OUTER_REST + k)
        value = jnp.sum(jnp.where(mask, outer, 0.0), axis=1, keepdims=True)
        result = jnp.where(r * RANK + s == k, value, result)
    core_out[...] = result


VMEM = pl.BlockSpec(memory_space=pltpu.VMEM)
HBM = pl.BlockSpec(memory_space=pltpu.HBM)


def call(kernel, name, outs, ins, flops, moved, scratch=(), limit=24):
    return pl.pallas_call(
        kernel,
        name=name,
        out_shape=outs,
        in_specs=ins,
        out_specs=jax.tree.map(lambda _: VMEM, outs),
        scratch_shapes=scratch,
        cost_estimate=pl.CostEstimate(flops=128 * flops, bytes_accessed=32 * moved, transcendentals=0),
        compiler_params=pltpu.CompilerParams(vmem_limit_bytes=limit << 20),
    )


def shape(dims, kind):
    return jax.ShapeDtypeStruct(dims, kind)


def local_pairs(grads, values, expand_weight, row_factors, col_factors, core, pair_index, counts):
    far = lax.axis_size("far")
    nmem = 2 * far
    tokens, depth = grads.shape
    vrows, width = values.shape
    rows = pair_index.shape[1]
    factors = NR * RANK + NC * RANK
    swap = [(0, 1), (1, 0)]

    def along_far(block, k):
        return lax.ppermute(block, "far", [(i, i ^ k) for i in range(far)])

    near_weight = lax.ppermute(expand_weight, "near", swap)
    blocks = [shape(((4 if k < WHOLE else 2) * rows + RECORD, 128), BF16) for k in range(far)]
    operands = (pair_index, counts.reshape(1, nmem), core, row_factors.T, col_factors.T, grads)
    *sends, scaled, hits = call(
        functools.partial(prepare_kernel, far),
        "prepare",
        (*blocks, shape((factors, rows), F32), shape((tokens, rows), BF16)),
        [HBM] * 6,
        rows * tokens * depth,
        2 * tokens * depth,
        [pltpu.VMEM(a.shape, a.dtype) for a in operands] + [pltpu.SemaphoreType.DMA((6,))],
    )(*(pltpu.with_memory_space_constraint(a, pltpu.HBM) for a in operands))
    got = {k: along_far(sends[k], k) for k in reversed(range(1, far))}
    ours = [sends[0]] + [got[k] for k in range(1, far)]
    theirs = [lax.ppermute(block, "col", swap) for block in ours[WHOLE:]]
    near_values = lax.ppermute(values, "near", swap)
    code = shape((2 * rows + RECORD, 128), jnp.int16)
    whole, *coded = call(
        functools.partial(project_kernel, far),
        "project",
        (shape((rows, width), F32),) + (code,) * (far - 1),
        [VMEM] * (2 * far - WHOLE + 2),
        4 * E * far * rows * depth // far * width,
        8 * E * width * depth // nmem,
    )(*ours, *theirs, expand_weight, near_weight)
    coded = [along_far(coded[j - 1], j) for j in reversed(range(1, far))]
    fetched, records, value_rows = call(
        functools.partial(lookup_kernel, far),
        "lookup",
        (shape((rows, width), F32), shape((rows, rows), F32), shape((8, rows), F32)),
        [VMEM] * (far + 2),
        2 * rows * vrows * width,
        4 * vrows * width,
    )(*ours, values, near_values)
    fars = sorted(range(far), key=lambda z: abs(2 * z - far))
    contrib, pass_on, back = call(
        functools.partial(reduce_kernel, far, fars),
        "reduce",
        (
            shape((rows // 2, width), BF16),
            shape((rows // 2 + RECORD, width), BF16),
            shape((2 * nmem, 1, rows), F32),
        ),
        [VMEM] * (3 + far),
        8 * rows * width,
        10 * rows * width,
    )(whole, fetched, records, value_rows, *coded)
    order = [4 * z + k for z in fars for k in (3, 2, 1, 0)]
    back = lax.all_to_all(
        back,
        ("far", "near", "col"),
        split_axis=0,
        concat_axis=0,
        axis_index_groups=[order],
        tiled=True,
    )
    passed = lax.ppermute(pass_on, "near", swap)
    value_grad, row_grad, col_grad, core_grad = call(
        functools.partial(output_kernel, far, order),
        "outputs",
        (
            shape((vrows, width), F32),
            shape((NR * RANK, tokens), F32),
            shape((NC * RANK, tokens), F32),
            shape((RANK, RANK), F32),
        ),
        [VMEM] * 6,
        2 * rows * vrows * width,
        4 * vrows * width,
    )(contrib, passed, value_rows, back, scaled, hits)
    return value_grad, row_grad.T, col_grad.T, core_grad


def solution(mesh):
    ngroup, nmem, ncol = (mesh.shape[a] for a in ("group", "mem", "col"))

    def run(*args):
        rows = args[6].shape[1] // (ngroup * nmem)
        depth = args[0].shape[1]
        fits = nmem % 2 == 0 and ncol == 2 and rows == 16 * nmem == 128
        fits = fits and depth == 256 * nmem and args[1].shape[1] == 256 * ncol
        if fits and nmem * rows <= E * depth:
            used = Mesh(
                mesh.devices.reshape(ngroup, nmem // 2, 2, ncol), ("group", "far", "near", "col")
            )
            mem, body = ("far", "near"), local_pairs
        else:
            used, mem, body = mesh, ("mem",), local_weights
        both = ("group",) + mem
        return jax.shard_map(
            body,
            mesh=used,
            in_specs=(
                P(both, None),
                P(mem, "col"),
                P(None, "col", mem),
                P(both, None),
                P(both, None),
                P(),
                P(None, both),
                P(both),
            ),
            out_specs=(
                P(both, "col"),
                P(both, None),
                P(both, None),
                P("group", None),
            ),
            check_vma=False,
        )(*args)

    return run
```
